256 devices in a mesh: grp: 8 (over z), seq: 16 (over y_hi, x, core), tp: 2 (over y_lo).
Axes of the slice: x: 4, y: 4 (y_hi: 2, y_lo: 2; y = y_hi * 2 + y_lo), z: 8, core: 2. Of those that a mesh axis runs over, the one named last changes fastest.
Arguments:
- token_ids: int32 [8, 128], replicated, may hold values from 0 to 32127
- text_lengths: int32 [8], P('grp'), may hold values from 32 to 128, as said below
- embed_table: bfloat16 [32128, 4096], P(('seq', 'tp'), 'grp'), may hold values from -36 to 36
- ff_gain: float32 [4096], P('grp'), may hold values from 0.5 to 1.5
- wi_gate: bfloat16 [4096, 10240], P('grp', ('seq', 'tp')), may hold values from -0.09375 to 0.09375
- wi_up: bfloat16 [4096, 10240], P('grp', ('seq', 'tp')), may hold values from -0.09375 to 0.09375
- wo_down: bfloat16 [10240, 4096], P(('seq', 'tp')), may hold values from -0.0625 to 0.0625
- final_gain: float32 [4096], P(('seq', 'tp')), may hold values from 0.5 to 1.5
- cap_weight: bfloat16 [4096, 1152], P(('seq', 'tp')), may hold values from -0.09375 to 0.09375
- cap_bias: float32 [1152], replicated, may hold values from -8 to 8
- image: bfloat16 [8, 6144, 1152], P('grp', ('seq', 'tp')), may hold values from -6 to 6
- modulation: float32 [8, 3, 1152], P('grp'), may hold values from -2 to 7
- w_qkv: bfloat16 [1152, 3456], P(None, 'seq'), may hold values from -0.1875 to 0.1875
- w_out: bfloat16 [1152, 1152], P(('seq', 'tp')), may hold values from -0.1875 to 0.1875
- w_cq: bfloat16 [1152, 1152], P(('seq', 'tp')), may hold values from -0.1875 to 0.1875
- w_ckv: bfloat16 [1152, 2304], P(None, ('seq', 'tp')), may hold values from -0.1875 to 0.1875
- w_co: bfloat16 [1152, 1152], P(('seq', 'tp')), may hold values from -0.1875 to 0.1875
Outputs:
- result: bfloat16 [8, 6144, 1152], P('grp', ('seq', 'tp'))
The draws below stay inside these ranges and needn't reach their ends.
Inputs may be any that keep to these rules, and one draw needn't show every extreme that they name: `text_lengths`: one prompt in every draw is unpadded.
All inputs are finite; a program needn't handle non-finite values.
Results may differ from the reference program's by a relative error of at most 0.014.
The reference program's roundings to bfloat16 on the way count: a program that leaves them out, or rounds other values in their place, can miss the bound.
Values may be sent and summed in bfloat16 or wider, within the bound.
No kernel may reach another device: no remote copies, remote signals or barrier semaphores. Data moves between devices by JAX's collectives and lax.ppermute only.
A program may use at most 128 MiB of HBM per device.

```python
import math
import jax
import jax.numpy as jnp
import numpy as np
from jax import lax

W = 1152
HEADS = 16
DT = 4096
FF_T = 10240
VOCAB = 32128
LT = 128
HEAD = 72
IMAGES = 8
IMG_TOK = 6144


def draw_text_lengths(key, part):
    key = jax.random.fold_in(key, 14)
    first_key, second_key = jax.random.split(key)
    drawn = jax.random.randint(first_key, (IMAGES,), LT // 4, LT + 1)
    chosen = jax.random.randint(second_key, (), 0, IMAGES)
    return jnp.where(jnp.arange(IMAGES) == chosen, LT, drawn).astype(jnp.int32)


def embed_columns(col_key, rise):
    position = jnp.arange(DT, dtype=jnp.float32) / max(DT - 1, 1)
    return rise ** position * jnp.exp(jax.random.uniform(col_key, (DT,), minval=-0.5, maxval=0.5))


def draw_embed_table(key, part):
    key = jax.random.fold_in(key, 11)
    col_key, row_key, base_key = jax.random.split(key, 3)
    row_scale = jnp.exp(jax.random.uniform(row_key, (VOCAB, 1), minval=-1.15, maxval=1.15))
    col_scale = embed_columns(col_key, 10.0)
    base = jnp.clip(jax.random.normal(base_key, (VOCAB, DT)), -3.0, 3.0)
    return (base * row_scale * col_scale * 0.15).astype(jnp.bfloat16)


def draw_cap_bias(key, part):
    key = jax.random.fold_in(key, 12)
    values = jnp.clip(jax.random.normal(key, (W,)) * 0.5, -2.0, 2.0)
    return values.astype(jnp.float32)


def draw_modulation(key, part):
    key = jax.random.fold_in(key, 13)
    shift_key, scale_key, gate_key = jax.random.split(key, 3)
    shifts = jnp.clip(jax.random.normal(shift_key, (IMAGES, W)) * 0.5, -2.0, 2.0)
    scales = jax.random.uniform(scale_key, (IMAGES, W), minval=-0.5, maxval=1.5)
    gates = jax.random.uniform(gate_key, (IMAGES, W), minval=0.5, maxval=1.5)
    return jnp.stack([shifts, scales, gates], axis=1).astype(jnp.float32)


def set_ends(entries, own_key, low, high):
    longest = entries.shape.index(max(entries.shape))
    spots = []
    for shift in (0, 1):
        where = [jax.random.randint(jax.random.fold_in(own_key, axis), (), 0, length) for axis, length in enumerate(entries.shape)]
        where[longest] = (where[longest] + shift) % entries.shape[longest]
        spots.append(tuple(where))
    return entries.at[spots[0]].set(low).at[spots[1]].set(high)


def level_of(own_key, shape, cuts, least, top_value):
    level = 1.0
    for axis_at, parts in cuts:
        steps = jax.random.uniform(jax.random.fold_in(jax.random.fold_in(own_key, 6), axis_at), (parts,), jnp.float32, least / len(cuts), top_value / len(cuts))
        level = level * jnp.repeat(jnp.exp(steps), shape[axis_at] // parts).reshape((-1,) + (1,) * (len(shape) - 1 - axis_at))
    return level


def cumulative_ranks(count, skew):
    loads = [(1 << 20) // math.isqrt(grade ** skew) + 1 for grade in range(1, count + 1)]
    width = 1 + sum(loads) // (1 << 30)
    return np.cumsum(np.array([max(1, weight // width) for weight in loads]))


def ranked(rng, shape, amount, slope):
    grid = cumulative_ranks(amount, slope)
    ticket = jax.random.randint(jax.random.fold_in(rng, 1), shape, 0, int(grid[amount - 1]))
    grade = jnp.searchsorted(jnp.asarray(grid, jnp.int32), ticket, side="right")
    return jax.random.permutation(jax.random.fold_in(rng, 2), amount)[grade].astype(jnp.int32)


def centred(stream_key, shape, deviation, most, shards=(), kind=jnp.bfloat16):
    values = deviation * jax.random.normal(stream_key, shape, jnp.float32)
    if shards:
        values = values * level_of(stream_key, shape, shards, -0.22, 0.18)
    return jnp.clip(values, -most, most).astype(kind)


def setup_inputs(seed: int = 0) -> dict:
    key_of = jax.random.split(jax.random.key(seed), 18)
    token_ids = set_ends(ranked(key_of[0], (IMAGES, LT), VOCAB, 2), jax.random.fold_in(key_of[0], 3), 0, VOCAB - 1).astype(jnp.int32)
    text_lengths = draw_text_lengths(jax.random.fold_in(key_of[17], 71), 0)
    embed_table = draw_embed_table(jax.random.fold_in(key_of[17], 71), 0)
    ff_gain = jnp.clip(1.0 + 0.1 * jax.random.normal(key_of[3], (DT,), jnp.float32), 0.5, 1.5)
    wi_gate = centred(key_of[4], (DT, FF_T), DT ** -0.5, 0.09375, ((0, 8), (1, 32)))
    wi_up = centred(key_of[5], (DT, FF_T), DT ** -0.5, 0.09375, ((0, 8), (1, 32)))
    wo_down = centred(key_of[6], (FF_T, DT), FF_T ** -0.5, 0.0625, ((0, 32),))
    final_gain = jnp.clip(1.0 + 0.1 * jax.random.normal(key_of[7], (DT,), jnp.float32), 0.5, 1.5)
    cap_weight = centred(key_of[8], (DT, W), DT ** -0.5, 0.09375, ((0, 32),))
    cap_bias = draw_cap_bias(jax.random.fold_in(key_of[17], 71), 0)
    image = centred(key_of[10], (IMAGES, IMG_TOK, W), 1.0, 6.0, ((0, 8), (1, 32)))
    modulation = draw_modulation(jax.random.fold_in(key_of[17], 71), 0)
    w_qkv = centred(key_of[12], (W, 3 * W), W ** -0.5, 0.1875, ((1, 16),))
    w_out = centred(key_of[13], (W, W), W ** -0.5, 0.1875, ((0, 32),))
    w_cq = centred(key_of[14], (W, W), W ** -0.5, 0.1875, ((0, 32),))
    w_ckv = centred(key_of[15], (W, 2 * W), W ** -0.5, 0.1875, ((1, 32),))
    w_co = centred(key_of[16], (W, W), W ** -0.5, 0.1875, ((0, 32),))
    return dict(token_ids=token_ids, text_lengths=text_lengths, embed_table=embed_table, ff_gain=ff_gain, wi_gate=wi_gate, wi_up=wi_up, wo_down=wo_down, final_gain=final_gain, cap_weight=cap_weight, cap_bias=cap_bias, image=image, modulation=modulation, w_qkv=w_qkv, w_out=w_out, w_cq=w_cq, w_ckv=w_ckv, w_co=w_co)


EPSILON = 1e-06

def gelu_tanh(values):
    return jax.nn.gelu(values, approximate=True)

def image_layer(pixels, modulate, text_kv, length, w_qkv, w_out, w_cq, w_co):
    count = pixels.shape[0]
    pixels32 = pixels.astype(jnp.float32)
    center = lax.optimization_barrier(jnp.mean(pixels32, axis=-1, keepdims=True))
    spread = lax.optimization_barrier(jnp.mean((pixels32 - center) ** 2, axis=-1, keepdims=True))
    modulated = ((pixels32 - center) * lax.rsqrt(spread + EPSILON) * (1.0 + modulate[1]) + modulate[0]).astype(jnp.bfloat16)
    packed_qkv = jnp.dot(modulated, w_qkv, preferred_element_type=jnp.float32).astype(jnp.bfloat16)
    packed_qkv = jnp.moveaxis(packed_qkv.reshape(count, HEADS, 3 * HEAD), 1, 0)
    score_scale = 1.0 / math.sqrt(HEAD)
    block_rows = math.gcd(count, 768)

    def one_head(head_pack):
        queries = head_pack[:, :HEAD].reshape(count // block_rows, block_rows, HEAD)
        key_rows = head_pack[:, HEAD:2 * HEAD]
        value_rows = head_pack[:, 2 * HEAD:]

        def attend(query_block):
            scores = jnp.dot(query_block, key_rows.T, preferred_element_type=jnp.float32) * score_scale
            weighting = jax.nn.softmax(scores, axis=-1).astype(jnp.bfloat16)
            return jnp.dot(weighting, value_rows, preferred_element_type=jnp.float32).astype(jnp.bfloat16)
        return lax.map(attend, queries).reshape(count, HEAD)
    attended = lax.map(one_head, packed_qkv)
    attended = jnp.moveaxis(attended, 0, 1).reshape(count, W)
    after_self = (pixels32 + modulate[2] * jnp.dot(attended, w_out, preferred_element_type=jnp.float32)).astype(jnp.bfloat16)
    cross_query = jnp.dot(after_self, w_cq, preferred_element_type=jnp.float32).astype(jnp.bfloat16)
    cross_query = cross_query.reshape(count, HEADS, HEAD)
    key_heads = text_kv[:, :W].reshape(LT, HEADS, HEAD)
    value_heads = text_kv[:, W:].reshape(LT, HEADS, HEAD)
    scores = jnp.einsum('qhd,khd->hqk', cross_query.astype(jnp.float32), key_heads.astype(jnp.float32)) * score_scale
    visible = jnp.arange(LT, dtype=jnp.int32) < length
    scores = jnp.where(visible[None, None, :], scores, -1e+30)
    cross_probs = jax.nn.softmax(scores, axis=-1).astype(jnp.bfloat16)
    cross_out = jnp.einsum('hqk,khd->qhd', cross_probs.astype(jnp.float32), value_heads.astype(jnp.float32))
    cross_out = cross_out.astype(jnp.bfloat16).reshape(count, W)
    final = after_self.astype(jnp.float32) + jnp.dot(cross_out, w_co, preferred_element_type=jnp.float32)
    return final.astype(jnp.bfloat16)

def reference(token_ids, text_lengths, embed_table, ff_gain, wi_gate, wi_up, wo_down, final_gain, cap_weight, cap_bias, image, modulation, w_qkv, w_out, w_cq, w_ckv, w_co):
    embedded = jnp.take(embed_table, token_ids.astype(jnp.int32), axis=0)
    embed32 = embedded.astype(jnp.float32).reshape(IMAGES * LT, DT)
    first_sq = lax.optimization_barrier(jnp.sum(embed32 * embed32, axis=-1, keepdims=True))
    normed = (embed32 * lax.rsqrt(first_sq / DT + EPSILON) * ff_gain).astype(jnp.bfloat16)
    gate_pre = jnp.dot(normed, wi_gate, preferred_element_type=jnp.float32)
    up_pre = jnp.dot(normed, wi_up, preferred_element_type=jnp.float32)
    hidden = (gelu_tanh(gate_pre) * up_pre).astype(jnp.bfloat16)
    text_state = embed32 + jnp.dot(hidden, wo_down, preferred_element_type=jnp.float32)
    second_sq = lax.optimization_barrier(jnp.sum(text_state * text_state, axis=-1, keepdims=True))
    text_out = (text_state * lax.rsqrt(second_sq / DT + EPSILON) * final_gain).astype(jnp.bfloat16)
    caption = gelu_tanh(jnp.dot(text_out, cap_weight, preferred_element_type=jnp.float32) + cap_bias).astype(jnp.bfloat16)
    text_kv = jnp.dot(caption, w_ckv, preferred_element_type=jnp.float32).astype(jnp.bfloat16)
    text_kv = text_kv.reshape(IMAGES, LT, 2 * W)

    def per_image(items):
        pixels, modulate, kv_rows, length = items
        return image_layer(pixels, modulate, kv_rows, length, w_qkv, w_out, w_cq, w_co)
    return lax.map(per_image, (image, modulation, text_kv, text_lengths.astype(jnp.int32)))
```

```python
import math

import jax
import jax.numpy as jnp
from jax import lax
from jax.experimental import pallas as pl
from jax.experimental.pallas import tpu as pltpu
from jax.sharding import Mesh
from jax.sharding import PartitionSpec as P

W = 1152
HEADS = 16
DT = 4096
HEAD = 72
SLOT = 80
PART = 36
GAP = 40
LT = 128
EPSILON = 1e-06
PLANE = ("yhi", "x", "core", "tp")
SEQ = ("yhi", "x", "core")
SIDE = ("yhi", "core")
SCORE_SCALE = 1.0 / math.sqrt(HEAD)
EXP2_SCALE = SCORE_SCALE * math.log2(math.e)
LIFT = 64.0
F32 = jnp.float32
BF16 = jnp.bfloat16

VMEM = pl.BlockSpec(memory_space=pltpu.VMEM)
SMEM = pl.BlockSpec(memory_space=pltpu.SMEM)


def grant(mib):
    return pltpu.CompilerParams(vmem_limit_bytes=mib * 1024 * 1024)


def gelu_tanh(values):
    return jax.nn.gelu(values, approximate=True)


def exchange(blocks, axes):
    return lax.all_to_all(blocks, axes, 0, 0, tiled=True)


def shifted(value, axis, shift):
    size = lax.axis_size(axis)
    return lax.ppermute(value, axis, [(i, (i + shift) % size) for i in range(size)])


def crossed(value, axis, mask):
    size = lax.axis_size(axis)
    return lax.ppermute(value, axis, [(i, i ^ mask) for i in range(size)])


def nt_dot(a, b):
    return lax.dot_general(a, b, (((1,), (1,)), ((), ())), preferred_element_type=F32)


def thirds(values):
    high = values.astype(BF16).astype(F32)
    mid = (values - high).astype(BF16).astype(F32)
    return high, mid, values - high - mid


TICK = (8, 128)


def call(
    kernel,
    name,
    out_shape,
    args,
    scratch=(),
    in_specs=None,
    flops=0,
    moved=1 << 20,
    exps=0,
    after=(),
    tick=False,
    mib=16,
):
    outs = list(out_shape) if isinstance(out_shape, list) else [out_shape]
    many = tick or isinstance(out_shape, list)
    if tick:
        outs.append(shape(TICK, F32))
    first, waits = len(args), len(after)
    last = first + waits + len(outs)

    def body(*refs):
        if tick:
            refs[last - 1][...] = jnp.zeros(TICK, F32)
        kernel(*refs[:first], *refs[first + waits : last - tick], *refs[last:])

    return pl.pallas_call(
        body,
        out_shape=outs if many else outs[0],
        in_specs=(in_specs or [VMEM] * len(args)) + [VMEM] * waits,
        out_specs=[VMEM] * len(outs) if many else VMEM,
        scratch_shapes=list(scratch),
        compiler_params=grant(mib),
        cost_estimate=pl.CostEstimate(flops=flops, bytes_accessed=moved, transcendentals=exps),
        name=name,
    )(*args, *after)


def tie(*arrays):
    total = jnp.zeros(TICK, F32)
    for array in arrays:
        total = total + array[: TICK[0], : TICK[1]].astype(F32)
    return total


def shape(dims, dtype=BF16):
    return jax.ShapeDtypeStruct(dims, dtype)


def embed_kernel(in_ref, out_ref):
    total = in_ref[0].astype(F32)
    for j in range(1, in_ref.shape[0]):
        total += in_ref[j].astype(F32)
    total = total.astype(BF16)
    for j in range(out_ref.shape[0]):
        out_ref[j] = total


def row_of(column):
    return jnp.broadcast_to(column, (column.shape[0], 128)).T[:1]


def column_of(row):
    return jnp.broadcast_to(row, (128, row.shape[1])).T[:, :1]


def gate_up_kernel(at_ref, in_ref, gain_ref, gate_ref, up_ref, out_ref, weight, rows32):
    prompts, _, both = out_ref.shape
    plane, group, feats = in_ref.shape
    tokens = plane * group // prompts
    share = tokens // plane
    weight[...] = (
        jnp.concatenate([gate_ref[...].astype(F32), up_ref[...].astype(F32)], axis=0)
        .T.astype(BF16)
    )
    per = plane // prompts
    at = at_ref[3] * share
    base = pl.multiple_of(at // 8 * 8, 8)
    upper = lax.rem(at, 8) == 0
    for p in range(prompts):
        rows = in_ref[p * per : (p + 1) * per].reshape(tokens, feats).astype(F32)
        rows32[...] = rows
        scaled = (rows * gain_ref[...]).astype(BF16)
        out_ref[p, :tokens, :] = jnp.dot(
            scaled, weight[...], preferred_element_type=F32
        ).astype(BF16)
        near = rows32[pl.ds(base, 8), :]
        own = jnp.where(upper, near[:share], near[share:])
        square = row_of(jnp.sum(rows * rows, axis=-1, keepdims=True))
        squares = jnp.concatenate(list(thirds(square)) + [jnp.zeros_like(square)], axis=0)
        out_ref[p, tokens:, :] = jnp.concatenate(
            [
                jnp.concatenate([own, jnp.zeros((share, both - feats), F32)], axis=1),
                jnp.concatenate([squares, jnp.zeros((4, both - tokens), F32)], axis=1),
            ],
            axis=0,
        ).astype(BF16)


def down_kernel(in_ref, down_ref, out_ref):
    groups, rows, both = in_ref.shape
    plane, _, width = out_ref.shape
    tokens = 128
    share = tokens // plane
    units = down_ref.shape[0]
    feats = DT // groups
    total = in_ref[0, :tokens, :].astype(F32)
    square = None
    for g in range(groups):
        if g:
            total += in_ref[g, :tokens, :].astype(F32)
        extra = in_ref[g, tokens:, :].astype(F32)
        for i in range(3):
            part = extra[share + i : share + i + 1, :tokens]
            square = part if square is None else square + part
        for k in range(feats // width):
            piece = extra[:share, k * width : (k + 1) * width]
            out_ref[g * (feats // width) + k, tokens:, :] = jnp.concatenate(
                [piece, jnp.zeros_like(piece)], axis=0
            ).astype(BF16)
    inverse = column_of(lax.rsqrt(square / DT + EPSILON))
    total = total * inverse
    hidden = (gelu_tanh(total[:, :units]) * total[:, units:]).astype(BF16)
    step = 4
    for j in range(0, plane, step):
        part = jnp.dot(
            hidden, down_ref[:, j * width : (j + step) * width], preferred_element_type=F32
        ).astype(BF16)
        for k in range(step):
            out_ref[j + k, :tokens, :] = part[:, k * width : (k + 1) * width]


def cap_kernel(in_ref, gain_ref, weight_ref, out_ref, rest, wide):
    plane, share, _ = out_ref.shape
    tokens = plane * share
    total = in_ref[0, :tokens, :].astype(F32)
    for j in range(1, plane):
        total += in_ref[j, :tokens, :].astype(F32)
    for j in range(plane):
        rest[j * share : (j + 1) * share, :] = in_ref[j, tokens:, :].astype(F32)[:share]
    state = total + rest[...]
    high, mid, low = thirds(jnp.sum(state * state, axis=-1, keepdims=True))
    lane = lax.broadcasted_iota(jnp.int32, (tokens, wide.shape[1] - W), 1)
    wide[:, W:] = jnp.where(
        lane == 0, high, jnp.where(lane == 1, mid, jnp.where(lane == 2, low, 0.0))
    )
    gained = (state * gain_ref[...]).astype(BF16)
    wide[:, :W] = jnp.dot(gained, weight_ref[...], preferred_element_type=F32)
    for j in range(plane):
        out_ref[j] = wide[j * share : (j + 1) * share, :].astype(BF16)


def caption_kernel(in_ref, bias_ref, out_ref):
    total = in_ref[0].astype(F32)
    for j in range(1, in_ref.shape[0]):
        total += in_ref[j].astype(F32)
    square = total[:, W : W + 1] + total[:, W + 1 : W + 2] + total[:, W + 2 : W + 3]
    inverse = lax.rsqrt(square / DT + EPSILON)
    caption = gelu_tanh(total[:, :W] * inverse + bias_ref[...]).astype(BF16)
    for j in range(out_ref.shape[0]):
        out_ref[j] = caption


def kv_kernel(in_ref, weight_ref, out_ref, rows):
    plane, share, _ = in_ref.shape
    for j in range(plane):
        rows[j * share : (j + 1) * share, :] = in_ref[j].astype(F32)
    kv = nt_dot(weight_ref[...], rows[...].astype(BF16)).astype(BF16)
    for j in range(plane):
        out_ref[j] = kv


def modulate_kernel(image_ref, mod_ref, out_ref):
    pixels = image_ref[...].astype(F32)
    center = jnp.mean(pixels, axis=-1, keepdims=True)
    spread = jnp.mean((pixels - center) ** 2, axis=-1, keepdims=True)
    out_ref[...] = (
        (pixels - center) * lax.rsqrt(spread + EPSILON) * (1.0 + mod_ref[1:2]) + mod_ref[0:1]
    ).astype(BF16)


def side_kernel(*refs):
    out_ref = refs[-1]
    zeros = jnp.zeros((GAP - PART, W), F32)
    for k, ref in enumerate(refs[:-1]):
        out_ref[:, k * W : (k + 1) * W] = jnp.concatenate(
            [ref[...].astype(F32), zeros], axis=0
        ).astype(BF16)


def gapped(rows):
    zeros = jnp.zeros((GAP - PART, rows.shape[1]), F32)
    pieces = []
    for j in range(rows.shape[0] // PART):
        pieces += [rows[j * PART : (j + 1) * PART], zeros]
    return jnp.concatenate(pieces, axis=0)


def qkv_kernel(at_ref, *refs):
    tokens, weights = refs[:4], refs[4:8]
    fulls, pairs = refs[8:12], refs[12:16]
    x_rows = refs[16]
    rows = tokens[0].shape[0]
    for m, block in enumerate(tokens):
        at = lax.rem(at_ref[1] - m + 4, 4)
        x_rows[pl.ds(pl.multiple_of(at * rows, rows), rows), :] = block[...]
    span = x_rows.shape[0]
    zeros = jnp.zeros((SLOT - HEAD, span), F32)
    ones = (lax.broadcasted_iota(jnp.int32, zeros.shape, 0) == 0).astype(F32)
    for s in range(4):
        out = nt_dot(weights[s][...], x_rows[...])
        slots = [
            jnp.concatenate([out[i * HEAD : (i + 1) * HEAD], tail], axis=0).astype(BF16)
            for i, tail in enumerate((zeros, ones, zeros))
        ]
        for i in range(3):
            fulls[s][i * SLOT : (i + 1) * SLOT, :] = slots[i]
        for i in range(2):
            pairs[s][i * SLOT : (i + 1) * SLOT, :] = slots[i + 1]


ROWS = 192
TILE = 256


def attention_kernel(at_ref, *refs):
    fulls, others = refs[:4], refs[4:8]
    outs = refs[8:10]
    keys, vals, qry, terms_a, terms_b, found = refs[10:16]
    span = fulls[0].shape[1]
    count = 8 * span
    largest = None
    for c, (ref, first) in enumerate([(r, SLOT) for r in fulls] + [(r, 0) for r in others]):
        block = ref[first : first + SLOT, :]
        cols = slice(c * span, (c + 1) * span)
        keys[:SLOT, cols] = block
        keys[SLOT:, cols] = block
        vals[cols, :] = ref[first + SLOT : first + 2 * SLOT, :].astype(F32).T.astype(BF16)
        wide = block.astype(F32)
        row = lax.broadcasted_iota(jnp.int32, wide.shape, 0)
        norm = jnp.sum(jnp.where(row < HEAD, wide * wide, 0.0), axis=0, keepdims=True)
        largest = norm if largest is None else jnp.maximum(largest, norm)
    largest = jnp.max(largest, axis=-1, keepdims=True)
    for s in range(2):
        q = fulls[s][0:SLOT, :].astype(F32) * SCORE_SCALE
        high = q.astype(BF16).astype(F32)
        row = lax.broadcasted_iota(jnp.int32, q.shape, 0)
        bound = jnp.sqrt(jnp.sum(q * q, axis=0, keepdims=True) * largest) * (1.0 + 2.0**-6)
        high = jnp.where(row == HEAD, LIFT * math.log(2.0) - bound, high)
        low = jnp.where(row == HEAD, 0.0, q - high)
        both = jnp.concatenate([high, low], axis=0).T
        for a in range(4):
            away = lax.rem(a - at_ref[1] + 4, 4)
            qry[s * 4 + away] = both[a * ROWS : (a + 1) * ROWS].astype(BF16)

    def tile(t):
        return slice(t * TILE, (t + 1) * TILE)

    def fill(q, t, terms, total, shift=None):
        s = jnp.dot(q, keys[:, tile(t)], preferred_element_type=F32)
        e = jnp.exp(s if shift is None else s - shift)
        terms[:, tile(t)] = e
        return total + (e[:, :128] + e[:, 128:])

    def weigh(t, terms, inverse, acc):
        p = (terms[:, tile(t)] * inverse).astype(BF16)
        return acc + jnp.dot(p, vals[tile(t), :], preferred_element_type=F32)

    def put(i, acc):
        found[i] = acc.T[:HEAD].astype(BF16)

    tiles = count // TILE
    none = jnp.zeros((ROWS, 128), F32)
    empty = jnp.zeros((ROWS, SLOT), F32)

    def step(i, seen):
        one, two = qry[2 * i], qry[2 * i + 1]
        total_a, total_b, acc_a, acc_b = none, none, empty, empty
        for t in range(tiles):
            total_a = fill(one, t, terms_a, total_a)
        total_a = jnp.sum(total_a, axis=-1, keepdims=True)
        inverse = 1.0 / total_a
        for t in range(tiles):
            total_b = fill(two, t, terms_b, total_b)
            acc_a = weigh(t, terms_a, inverse, acc_a)
        put(2 * i, acc_a)
        total_b = jnp.sum(total_b, axis=-1, keepdims=True)
        inverse = 1.0 / total_b
        for t in range(tiles):
            acc_b = weigh(t, terms_b, inverse, acc_b)
        put(2 * i + 1, acc_b)
        least, most = seen
        return (
            jnp.minimum(least, jnp.min(jnp.minimum(total_a, total_b))),
            jnp.maximum(most, jnp.max(jnp.maximum(total_a, total_b))),
        )

    least, most = lax.fori_loop(0, 4, step, (jnp.float32(1.0), jnp.float32(1.0)))
    safe = jnp.logical_and(least > 2.0**-76, most < 2.0**100)

    @pl.when(jnp.logical_not(safe))
    def _():
        def again(i, _):
            q = qry[i].astype(F32)
            lane = lax.broadcasted_iota(jnp.int32, q.shape, 1)
            q = jnp.where(lane == HEAD, 0.0, q).astype(BF16)
            top = None
            for t in range(tiles):
                s = jnp.dot(q, keys[:, tile(t)], preferred_element_type=F32)
                here = jnp.max(s, axis=-1, keepdims=True)
                top = here if top is None else jnp.maximum(top, here)
            total = none
            for t in range(tiles):
                total = fill(q, t, terms_a, total, top)
            inverse = 1.0 / jnp.sum(total, axis=-1, keepdims=True)
            acc = empty
            for t in range(tiles):
                acc = weigh(t, terms_a, inverse, acc)
            put(i, acc)
            return 0

        lax.fori_loop(0, 8, again, 0)

    for s, out in enumerate(outs):
        out[...] = found[4 * s : 4 * s + 4]


def regroup_kernel(*refs):
    for m, out in enumerate(refs[4:]):
        for s, part in enumerate(refs[:4]):
            out[s] = part[m]


def project_kernel(at_ref, *refs):
    parts = refs[:4]
    wout_ref, wcq_ref, img_ref, gate_ref, after_ref, cq_ref, tick_ref, wide = refs[4:]
    tick_ref[...] = jnp.zeros(TICK, F32)
    for d, part in enumerate(parts):
        x = lax.rem(at_ref[1] - d + 4, 4)
        for m in range(4):
            side = lax.bitwise_xor(at_ref[0], m)
            head = (side // 2) * 8 + x * 2 + lax.rem(side, 2)
            wide[pl.ds(pl.multiple_of(head * 2 * GAP, 16), 2 * GAP), :] = gapped(
                part[m].astype(F32)
            )
    projected = jnp.dot(wide[...].T.astype(BF16), wout_ref[...], preferred_element_type=F32)
    after = (img_ref[...].astype(F32) + gate_ref[...] * projected).astype(BF16)
    after_ref[...] = after
    query = gapped(after.astype(F32).T).T.astype(BF16)
    cq_ref[...] = jnp.dot(query, wcq_ref[...], preferred_element_type=F32).astype(BF16)


def cross_kernel(len_ref, cq_ref, after_ref, kv_ref, wco_ref, out_ref, wide):
    length = len_ref[0]
    rows = cq_ref.shape[0]
    visible = lax.broadcasted_iota(jnp.int32, (rows, LT), 1) < length
    for h in range(HEADS):
        qry = cq_ref[:, h * HEAD : (h + 1) * HEAD]
        s = jnp.dot(qry, kv_ref[h], preferred_element_type=F32) * SCORE_SCALE
        s = jnp.where(visible, s, -1e30)
        e = jnp.exp(s - jnp.max(s, axis=-1, keepdims=True))
        p = (e / jnp.sum(e, axis=-1, keepdims=True)).astype(BF16)
        wide[h * 2 * GAP : (h + 1) * 2 * GAP, :] = gapped(nt_dot(kv_ref[HEADS + h], p))
    final = jnp.dot(wide[...].T.astype(BF16), wco_ref[...], preferred_element_type=F32)
    out_ref[...] = (after_ref[...].astype(F32) + final).astype(BF16)


def whole(dims):
    return pl.BlockSpec(dims, lambda i: (0,) * len(dims))


def third(k):
    return pl.BlockSpec((W // PART * GAP, W), lambda i: (0, k))


def project(at, parts, side, img, gate):
    rows = img.shape[0]
    return pl.pallas_call(
        project_kernel,
        grid=(1,),
        out_shape=[shape((rows, W))] * 2 + [shape(TICK, F32)],
        in_specs=[SMEM]
        + [whole(part.shape) for part in parts]
        + [third(0), third(1), whole(img.shape), whole(gate.shape)],
        out_specs=[whole((rows, W))] * 2 + [whole(TICK)],
        scratch_shapes=[pltpu.VMEM((W // PART * GAP, rows), F32)],
        compiler_params=grant(56),
        cost_estimate=pl.CostEstimate(
            flops=4 * rows * W * W, bytes_accessed=8 << 20, transcendentals=0
        ),
        name="project_out_and_query",
    )(at, *parts, side, side, img, gate)


def cross(length, cq, after, kv, side):
    rows = cq.shape[0]
    return pl.pallas_call(
        cross_kernel,
        grid=(1,),
        out_shape=shape((rows, W)),
        in_specs=[SMEM, whole(cq.shape), whole(after.shape), whole(kv.shape), third(2)],
        out_specs=whole((rows, W)),
        scratch_shapes=[pltpu.VMEM((W // PART * GAP, rows), F32)],
        compiler_params=grant(56),
        cost_estimate=pl.CostEstimate(
            flops=4 * rows * W * W, bytes_accessed=5 << 20, transcendentals=rows * LT * HEADS
        ),
        name="cross_attention",
    )(length, cq, after, kv, side)


def local(
    token_ids,
    text_lengths,
    embed_table,
    ff_gain,
    wi_gate,
    wi_up,
    wo_down,
    final_gain,
    cap_weight,
    cap_bias,
    image,
    modulation,
    w_qkv,
    w_out,
    w_cq,
    w_ckv,
    w_co,
):
    plane = lax.axis_size(PLANE)
    place = lax.axis_index(PLANE)
    prompts, tokens = token_ids.shape
    share = tokens // plane
    vocab_rows, feats = embed_table.shape
    units = wi_gate.shape[1]
    width = DT // plane

    local_ids = token_ids.reshape(-1) - place * vocab_rows
    one_hot = (local_ids[:, None] == jnp.arange(vocab_rows, dtype=jnp.int32)[None]).astype(BF16)
    picked = jnp.dot(one_hot, embed_table, preferred_element_type=F32).astype(BF16)
    picked = exchange(picked.reshape(plane, -1, feats), PLANE)

    pixels = image[0]
    rows = pixels.shape[0]
    modulate = modulation[0]
    modulated = call(modulate_kernel, "modulate", shape((rows, W)), (pixels, modulate))
    token_blocks = [modulated] + [shifted(modulated, "x", s) for s in range(1, 4)]
    weight_blocks = [w_qkv.T] + [crossed(w_qkv.T, SIDE, m) for m in range(1, 4)]
    at = jnp.stack([lax.axis_index(a) for a in (SIDE, "x", "tp", PLANE)]).astype(jnp.int32)
    span = 4 * rows
    made = call(
        qkv_kernel,
        "query_key_value",
        [shape((3 * SLOT, span))] * 4 + [shape((2 * SLOT, span))] * 4,
        (at, *token_blocks, *weight_blocks),
        scratch=[pltpu.VMEM((span, W), BF16)],
        in_specs=[SMEM] + [VMEM] * 8,
        flops=2 * span * W * 12 * HEAD,
        moved=8 << 20,
        mib=56,
    )
    fulls = [made[0]] + [crossed(made[m], SIDE, m) for m in range(1, 4)]
    others = [crossed(made[4 + m], SIDE + ("tp",), 2 * m + 1) for m in range(4)]

    def attend(first, after):
        found = call(
            attention_kernel,
            "self_attention",
            [shape((4, HEAD, rows))] * 2,
            (at, *(fulls[(first + s) % 4] for s in range(4)), *others),
            scratch=[
                pltpu.VMEM((2 * SLOT, 8 * span), BF16),
                pltpu.VMEM((8 * span, SLOT), BF16),
                pltpu.VMEM((8, ROWS, 2 * SLOT), BF16),
                pltpu.VMEM((ROWS, 8 * span), F32),
                pltpu.VMEM((ROWS, 8 * span), F32),
                pltpu.VMEM((8, HEAD, ROWS), BF16),
            ],
            in_specs=[SMEM] + [VMEM] * 8,
            flops=8 * span * 2 * span * 256 * 2,
            moved=8 << 20,
            exps=2 * span * 8 * span,
            after=after,
            tick=True,
            mib=56,
        )
        parts = [
            crossed(part, SIDE, first + m) if first + m else part
            for m, part in enumerate(found[:2])
        ]
        return parts, found[2:]

    embedded, tick = call(
        embed_kernel,
        "embed_sum",
        [shape(picked.shape)],
        (picked,),
        after=(tie(*token_blocks[1:], *weight_blocks[1:]),),
        tick=True,
    )
    side = call(side_kernel, "side_weights", shape((GAP, 3 * W)), (w_out, w_cq, w_co), after=(tick,))
    side = lax.all_gather(side, PLANE, axis=0, tiled=True)
    gate_up, tick = call(
        gate_up_kernel,
        "text_gate_up",
        shape((prompts, tokens + 2 * share, 2 * units)),
        (at, exchange(embedded, PLANE), ff_gain.reshape(1, feats), wi_gate.T, wi_up.T),
        scratch=[pltpu.VMEM((feats, 2 * units), BF16), pltpu.VMEM((tokens, feats), F32)],
        in_specs=[SMEM] + [VMEM] * 4,
        flops=4 * prompts * tokens * feats * units,
        moved=4 << 20,
        after=(tie(*fulls[1:], *others),),
        tick=True,
    )
    near, near_tick = attend(0, (tick,))
    far, far_tick = attend(2, near_tick)
    down = call(
        down_kernel,
        "text_down",
        shape((plane, tokens + 2 * share, width)),
        (exchange(gate_up, "grp"), wo_down),
        flops=2 * tokens * DT * units,
        moved=5 << 20,
        exps=tokens * units,
        after=far_tick,
    )
    *grouped, regroup_tick = call(
        regroup_kernel, "regroup", [shape((4, HEAD, rows))] * 4, (*near, *far), tick=True
    )
    cap_part = call(
        cap_kernel,
        "caption_partial",
        shape((plane, share, W + 128)),
        (exchange(down, PLANE), final_gain.reshape(1, width), cap_weight),
        scratch=[pltpu.VMEM((tokens, width), F32), pltpu.VMEM((tokens, W + 128), F32)],
        after=(regroup_tick,),
    )
    caption = call(
        caption_kernel,
        "caption",
        shape((plane, share, W)),
        (exchange(cap_part, PLANE), cap_bias.reshape(1, W)),
    )
    parts = [grouped[0]] + [shifted(grouped[d], "x", d) for d in range(1, 4)]
    after_self, cross_query, tick = project(at, parts, side, pixels, modulate[2:3])
    kv_part = call(
        kv_kernel,
        "text_kv",
        shape((plane, w_ckv.shape[1], tokens)),
        (exchange(caption, PLANE), w_ckv.T),
        scratch=[pltpu.VMEM((tokens, W), F32)],
        after=(tick,),
    )
    text_kv = exchange(kv_part, PLANE)
    result = cross(text_lengths, cross_query, after_self, text_kv, side)
    return result[None]


def solution(mesh):
    grp, seq, tp = mesh.devices.shape
    fine = Mesh(mesh.devices.reshape(grp, 2, seq // 4, 2, tp), ("grp",) + PLANE)
    placed = (
        P(),
        P("grp"),
        P(PLANE, "grp"),
        P("grp"),
        P("grp", PLANE),
        P("grp", PLANE),
        P(PLANE, None),
        P(PLANE),
        P(PLANE, None),
        P(),
        P("grp", PLANE, None),
        P("grp", None, None),
        P(None, SEQ),
        P(PLANE, None),
        P(PLANE, None),
        P(None, PLANE),
        P(PLANE, None),
    )
    return jax.shard_map(
        local, mesh=fine, in_specs=placed, out_specs=P("grp", PLANE, None), check_vma=False
    )
```

```python
import math

import jax
import jax.numpy as jnp
from jax import lax
from jax.experimental import pallas as pl
from jax.experimental.pallas import tpu as pltpu
from jax.sharding import Mesh
from jax.sharding import PartitionSpec as P

W = 1152
HEADS = 16
DT = 4096
HEAD = 72
SLOT = 80
LT = 128
EPSILON = 1e-06
PLANE = ("yhi", "x", "core", "tp")
SEQ = ("yhi", "x", "core")
SIDE = ("yhi", "core")
SCORE_SCALE = 1.0 / math.sqrt(HEAD)
EXP2_SCALE = SCORE_SCALE * math.log2(math.e)
LIFT = 64.0
F32 = jnp.float32
BF16 = jnp.bfloat16

VMEM = pl.BlockSpec(memory_space=pltpu.VMEM)
SMEM = pl.BlockSpec(memory_space=pltpu.SMEM)


def grant(mib):
    return pltpu.CompilerParams(vmem_limit_bytes=mib * 1024 * 1024)


def gelu_tanh(values):
    return jax.nn.gelu(values, approximate=True)


def exchange(blocks, axes):
    return lax.all_to_all(blocks, axes, 0, 0, tiled=True)


def shifted(value, axis, shift):
    size = lax.axis_size(axis)
    return lax.ppermute(value, axis, [(i, (i + shift) % size) for i in range(size)])


def crossed(value, axis, mask):
    size = lax.axis_size(axis)
    return lax.ppermute(value, axis, [(i, i ^ mask) for i in range(size)])


def nt_dot(a, b):
    return lax.dot_general(a, b, (((1,), (1,)), ((), ())), preferred_element_type=F32)


def thirds(values):
    high = values.astype(BF16).astype(F32)
    mid = (values - high).astype(BF16).astype(F32)
    return high, mid, values - high - mid


TICK = (8, 128)


def call(
    kernel,
    name,
    out_shape,
    args,
    scratch=(),
    in_specs=None,
    flops=0,
    moved=1 << 20,
    exps=0,
    after=(),
    tick=False,
    mib=16,
):
    outs = list(out_shape) if isinstance(out_shape, list) else [out_shape]
    many = tick or isinstance(out_shape, list)
    if tick:
        outs.append(shape(TICK, F32))
    first, waits = len(args), len(after)
    last = first + waits + len(outs)

    def body(*refs):
        if tick:
            refs[last - 1][...] = jnp.zeros(TICK, F32)
        kernel(*refs[:first], *refs[first + waits : last - tick], *refs[last:])

    return pl.pallas_call(
        body,
        out_shape=outs if many else outs[0],
        in_specs=(in_specs or [VMEM] * len(args)) + [VMEM] * waits,
        out_specs=[VMEM] * len(outs) if many else VMEM,
        scratch_shapes=list(scratch),
        compiler_params=grant(mib),
        cost_estimate=pl.CostEstimate(flops=flops, bytes_accessed=moved, transcendentals=exps),
        name=name,
    )(*args, *after)


def tie(*arrays):
    total = jnp.zeros(TICK, F32)
    for array in arrays:
        total = total + array[: TICK[0], : TICK[1]].astype(F32)
    return total


def shape(dims, dtype=BF16):
    return jax.ShapeDtypeStruct(dims, dtype)


def embed_kernel(in_ref, out_ref):
    total = in_ref[0].astype(F32)
    for j in range(1, in_ref.shape[0]):
        total += in_ref[j].astype(F32)
    total = total.astype(BF16)
    for j in range(out_ref.shape[0]):
        out_ref[j] = total


def row_of(column):
    return jnp.broadcast_to(column, (column.shape[0], 128)).T[:1]


def column_of(row):
    return jnp.broadcast_to(row, (128, row.shape[1])).T[:, :1]


def gate_up_kernel(at_ref, in_ref, gain_ref, gate_ref, up_ref, out_ref, weight, rows32):
    prompts, _, both = out_ref.shape
    plane, group, feats = in_ref.shape
    tokens = plane * group // prompts
    share = tokens // plane
    weight[...] = (
        jnp.concatenate([gate_ref[...].astype(F32), up_ref[...].astype(F32)], axis=0)
        .T.astype(BF16)
    )
    per = plane // prompts
    at = at_ref[3] * share
    base = pl.multiple_of(at // 8 * 8, 8)
    upper = lax.rem(at, 8) == 0
    for p in range(prompts):
        rows = in_ref[p * per : (p + 1) * per].reshape(tokens, feats).astype(F32)
        rows32[...] = rows
        scaled = (rows * gain_ref[...]).astype(BF16)
        out_ref[p, :tokens, :] = jnp.dot(
            scaled, weight[...], preferred_element_type=F32
        ).astype(BF16)
        near = rows32[pl.ds(base, 8), :]
        own = jnp.where(upper, near[:share], near[share:])
        square = row_of(jnp.sum(rows * rows, axis=-1, keepdims=True))
        squares = jnp.concatenate(list(thirds(square)) + [jnp.zeros_like(square)], axis=0)
        out_ref[p, tokens:, :] = jnp.concatenate(
            [
                jnp.concatenate([own, jnp.zeros((share, both - feats), F32)], axis=1),
                jnp.concatenate([squares, jnp.zeros((4, both - tokens), F32)], axis=1),
            ],
            axis=0,
        ).astype(BF16)


def down_kernel(in_ref, down_ref, out_ref):
    groups, rows, both = in_ref.shape
    plane, _, width = out_ref.shape
    tokens = 128
    share = tokens // plane
    units = down_ref.shape[0]
    feats = DT // groups
    total = in_ref[0, :tokens, :].astype(F32)
    square = None
    for g in range(groups):
        if g:
            total += in_ref[g, :tokens, :].astype(F32)
        extra = in_ref[g, tokens:, :].astype(F32)
        for i in range(3):
            part = extra[share + i : share + i + 1, :tokens]
            square = part if square is None else square + part
        for k in range(feats // width):
            piece = extra[:share, k * width : (k + 1) * width]
            out_ref[g * (feats // width) + k, tokens:, :] = jnp.concatenate(
                [piece, jnp.zeros_like(piece)], axis=0
            ).astype(BF16)
    inverse = column_of(lax.rsqrt(square / DT + EPSILON))
    total = total * inverse
    hidden = (gelu_tanh(total[:, :units]) * total[:, units:]).astype(BF16)
    step = 4
    for j in range(0, plane, step):
        part = jnp.dot(
            hidden, down_ref[:, j * width : (j + step) * width], preferred_element_type=F32
        ).astype(BF16)
        for k in range(step):
            out_ref[j + k, :tokens, :] = part[:, k * width : (k + 1) * width]


def cap_kernel(in_ref, gain_ref, weight_ref, out_ref, rest, wide):
    plane, share, _ = out_ref.shape
    tokens = plane * share
    total = in_ref[0, :tokens, :].astype(F32)
    for j in range(1, plane):
        total += in_ref[j, :tokens, :].astype(F32)
    for j in range(plane):
        rest[j * share : (j + 1) * share, :] = in_ref[j, tokens:, :].astype(F32)[:share]
    state = total + rest[...]
    high, mid, low = thirds(jnp.sum(state * state, axis=-1, keepdims=True))
    lane = lax.broadcasted_iota(jnp.int32, (tokens, wide.shape[1] - W), 1)
    wide[:, W:] = jnp.where(
        lane == 0, high, jnp.where(lane == 1, mid, jnp.where(lane == 2, low, 0.0))
    )
    gained = (state * gain_ref[...]).astype(BF16)
    wide[:, :W] = jnp.dot(gained, weight_ref[...], preferred_element_type=F32)
    for j in range(plane):
        out_ref[j] = wide[j * share : (j + 1) * share, :].astype(BF16)


def caption_kernel(in_ref, bias_ref, out_ref):
    total = in_ref[0].astype(F32)
    for j in range(1, in_ref.shape[0]):
        total += in_ref[j].astype(F32)
    square = total[:, W : W + 1] + total[:, W + 1 : W + 2] + total[:, W + 2 : W + 3]
    inverse = lax.rsqrt(square / DT + EPSILON)
    caption = gelu_tanh(total[:, :W] * inverse + bias_ref[...]).astype(BF16)
    for j in range(out_ref.shape[0]):
        out_ref[j] = caption


def kv_kernel(in_ref, weight_ref, out_ref, rows):
    plane, share, _ = in_ref.shape
    for j in range(plane):
        rows[j * share : (j + 1) * share, :] = in_ref[j].astype(F32)
    kv = nt_dot(weight_ref[...], rows[...].astype(BF16)).astype(BF16)
    for j in range(plane):
        out_ref[j] = kv


def modulate_kernel(image_ref, mod_ref, out_ref):
    pixels = image_ref[...].astype(F32)
    center = jnp.mean(pixels, axis=-1, keepdims=True)
    spread = jnp.mean((pixels - center) ** 2, axis=-1, keepdims=True)
    out_ref[...] = (
        (pixels - center) * lax.rsqrt(spread + EPSILON) * (1.0 + mod_ref[1:2]) + mod_ref[0:1]
    ).astype(BF16)


def side_kernel(*refs):
    out_ref = refs[-1]
    for k, ref in enumerate(refs[:-1]):
        out_ref[:, k * W : (k + 1) * W] = ref[...]


def pair_kernel(at_ref, own_ref, other_ref, out_ref):
    own, other = own_ref[...].astype(F32), other_ref[...].astype(F32)
    first = at_ref[2] == 0
    out_ref[...] = jnp.concatenate(
        [jnp.where(first, own, other), jnp.where(first, other, own)], axis=0
    ).astype(BF16)


def qkv_kernel(at_ref, *refs):
    tokens, weights = refs[:4], refs[4:8]
    fulls, pairs = refs[8:12], refs[12:16]
    x_rows = refs[16]
    rows = tokens[0].shape[0]
    for m, block in enumerate(tokens):
        at = lax.rem(at_ref[1] - m + 4, 4)
        x_rows[pl.ds(pl.multiple_of(at * rows, rows), rows), :] = block[...]
    span = x_rows.shape[0]
    zeros = jnp.zeros((SLOT - HEAD, span), F32)
    ones = (lax.broadcasted_iota(jnp.int32, zeros.shape, 0) == 0).astype(F32)
    for s in range(4):
        out = nt_dot(weights[s][...], x_rows[...])
        slots = [
            jnp.concatenate([out[i * HEAD : (i + 1) * HEAD], tail], axis=0).astype(BF16)
            for i, tail in enumerate((zeros, ones, zeros))
        ]
        for i in range(3):
            fulls[s][i * SLOT : (i + 1) * SLOT, :] = slots[i]
        for i in range(2):
            pairs[s][i * SLOT : (i + 1) * SLOT, :] = slots[i + 1]


ROWS = 192
TILE = 256


def attention_kernel(at_ref, *refs):
    fulls, others = refs[:4], refs[4:8]
    outs = refs[8:10]
    keys, vals, qry, terms_a, terms_b, found = refs[10:16]
    span = fulls[0].shape[1]
    count = 8 * span
    largest = None
    for c, (ref, first) in enumerate([(r, SLOT) for r in fulls] + [(r, 0) for r in others]):
        block = ref[first : first + SLOT, :]
        cols = slice(c * span, (c + 1) * span)
        keys[:SLOT, cols] = block
        keys[SLOT:, cols] = block
        vals[cols, :] = ref[first + SLOT : first + 2 * SLOT, :].astype(F32).T.astype(BF16)
        wide = block.astype(F32)
        row = lax.broadcasted_iota(jnp.int32, wide.shape, 0)
        norm = jnp.sum(jnp.where(row < HEAD, wide * wide, 0.0), axis=0, keepdims=True)
        largest = norm if largest is None else jnp.maximum(largest, norm)
    largest = jnp.max(largest, axis=-1, keepdims=True)
    for s in range(2):
        q = fulls[s][0:SLOT, :].astype(F32) * SCORE_SCALE
        high = q.astype(BF16).astype(F32)
        row = lax.broadcasted_iota(jnp.int32, q.shape, 0)
        bound = jnp.sqrt(jnp.sum(q * q, axis=0, keepdims=True) * largest) * (1.0 + 2.0**-6)
        high = jnp.where(row == HEAD, LIFT * math.log(2.0) - bound, high)
        low = jnp.where(row == HEAD, 0.0, q - high)
        both = jnp.concatenate([high, low], axis=0).T
        for a in range(4):
            away = lax.rem(a - at_ref[1] + 4, 4)
            qry[s * 4 + away] = both[a * ROWS : (a + 1) * ROWS].astype(BF16)

    def tile(t):
        return slice(t * TILE, (t + 1) * TILE)

    def fill(q, t, terms, total, shift=None):
        s = jnp.dot(q, keys[:, tile(t)], preferred_element_type=F32)
        e = jnp.exp(s if shift is None else s - shift)
        terms[:, tile(t)] = e
        return total + (e[:, :128] + e[:, 128:])

    def weigh(t, terms, inverse, acc):
        p = (terms[:, tile(t)] * inverse).astype(BF16)
        return acc + jnp.dot(p, vals[tile(t), :], preferred_element_type=F32)

    def put(i, acc):
        found[i] = acc.T[:HEAD].astype(BF16)

    tiles = count // TILE
    none = jnp.zeros((ROWS, 128), F32)
    empty = jnp.zeros((ROWS, SLOT), F32)

    def step(i, seen):
        one, two = qry[2 * i], qry[2 * i + 1]
        total_a, total_b, acc_a, acc_b = none, none, empty, empty
        for t in range(tiles):
            total_a = fill(one, t, terms_a, total_a)
        total_a = jnp.sum(total_a, axis=-1, keepdims=True)
        inverse = 1.0 / total_a
        for t in range(tiles):
            total_b = fill(two, t, terms_b, total_b)
            acc_a = weigh(t, terms_a, inverse, acc_a)
        put(2 * i, acc_a)
        total_b = jnp.sum(total_b, axis=-1, keepdims=True)
        inverse = 1.0 / total_b
        for t in range(tiles):
            acc_b = weigh(t, terms_b, inverse, acc_b)
        put(2 * i + 1, acc_b)
        least, most = seen
        return (
            jnp.minimum(least, jnp.min(jnp.minimum(total_a, total_b))),
            jnp.maximum(most, jnp.max(jnp.maximum(total_a, total_b))),
        )

    least, most = lax.fori_loop(0, 4, step, (jnp.float32(1.0), jnp.float32(1.0)))
    safe = jnp.logical_and(least > 2.0**-76, most < 2.0**100)

    @pl.when(jnp.logical_not(safe))
    def _():
        def again(i, _):
            q = qry[i].astype(F32)
            lane = lax.broadcasted_iota(jnp.int32, q.shape, 1)
            q = jnp.where(lane == HEAD, 0.0, q).astype(BF16)
            top = None
            for t in range(tiles):
                s = jnp.dot(q, keys[:, tile(t)], preferred_element_type=F32)
                here = jnp.max(s, axis=-1, keepdims=True)
                top = here if top is None else jnp.maximum(top, here)
            total = none
            for t in range(tiles):
                total = fill(q, t, terms_a, total, top)
            inverse = 1.0 / jnp.sum(total, axis=-1, keepdims=True)
            acc = empty
            for t in range(tiles):
                acc = weigh(t, terms_a, inverse, acc)
            put(i, acc)
            return 0

        lax.fori_loop(0, 8, again, 0)

    for s, out in enumerate(outs):
        out[...] = found[4 * s : 4 * s + 4]


def regroup_kernel(*refs):
    for m, out in enumerate(refs[4:]):
        for s, part in enumerate(refs[:4]):
            out[s] = part[m]


def project_kernel(at_ref, *refs):
    parts = refs[:4]
    wout_ref, wcq_ref, img_ref, gate_ref, after_ref, cq_ref, wide = refs[4:]
    for d, part in enumerate(parts):
        x = lax.rem(at_ref[1] - d + 4, 4)
        for m in range(4):
            side = lax.bitwise_xor(at_ref[0], m)
            head = (side // 2) * 8 + x * 2 + lax.rem(side, 2)
            wide[pl.ds(pl.multiple_of(head * HEAD, 8), HEAD), :] = part[m].astype(F32)
    projected = jnp.dot(wide[...].T.astype(BF16), wout_ref[...], preferred_element_type=F32)
    after = (img_ref[...].astype(F32) + gate_ref[...] * projected).astype(BF16)
    after_ref[...] = after
    cq_ref[...] = jnp.dot(after, wcq_ref[...], preferred_element_type=F32).astype(BF16)


def cross_kernel(len_ref, cq_ref, after_ref, kv_ref, wco_ref, out_ref, wide):
    length = len_ref[0]
    rows = cq_ref.shape[0]
    visible = lax.broadcasted_iota(jnp.int32, (rows, LT), 1) < length
    for h in range(HEADS):
        qry = cq_ref[:, h * HEAD : (h + 1) * HEAD]
        s = jnp.dot(qry, kv_ref[h], preferred_element_type=F32) * SCORE_SCALE
        s = jnp.where(visible, s, -1e30)
        e = jnp.exp(s - jnp.max(s, axis=-1, keepdims=True))
        p = (e / jnp.sum(e, axis=-1, keepdims=True)).astype(BF16)
        wide[h * HEAD : (h + 1) * HEAD, :] = nt_dot(kv_ref[HEADS + h], p)
    final = jnp.dot(wide[...].T.astype(BF16), wco_ref[...], preferred_element_type=F32)
    out_ref[...] = (after_ref[...].astype(F32) + final).astype(BF16)


def whole(dims):
    return pl.BlockSpec(dims, lambda i: (0,) * len(dims))


def third(k):
    return pl.BlockSpec((W, W), lambda i: (0, k))


def project(at, parts, side, img, gate):
    rows = img.shape[0]
    return pl.pallas_call(
        project_kernel,
        grid=(1,),
        out_shape=[shape((rows, W))] * 2,
        in_specs=[SMEM]
        + [whole(part.shape) for part in parts]
        + [third(0), third(1), whole(img.shape), whole(gate.shape)],
        out_specs=[whole((rows, W))] * 2,
        scratch_shapes=[pltpu.VMEM((W, rows), F32)],
        compiler_params=grant(56),
        cost_estimate=pl.CostEstimate(
            flops=4 * rows * W * W, bytes_accessed=8 << 20, transcendentals=0
        ),
        name="project_out_and_query",
    )(at, *parts, side, side, img, gate)


def cross(length, cq, after, kv, side):
    rows = cq.shape[0]
    return pl.pallas_call(
        cross_kernel,
        grid=(1,),
        out_shape=shape((rows, W)),
        in_specs=[SMEM, whole(cq.shape), whole(after.shape), whole(kv.shape), third(2)],
        out_specs=whole((rows, W)),
        scratch_shapes=[pltpu.VMEM((W, rows), F32)],
        compiler_params=grant(56),
        cost_estimate=pl.CostEstimate(
            flops=4 * rows * W * W, bytes_accessed=5 << 20, transcendentals=rows * LT * HEADS
        ),
        name="cross_attention",
    )(length, cq, after, kv, side)


def local(
    token_ids,
    text_lengths,
    embed_table,
    ff_gain,
    wi_gate,
    wi_up,
    wo_down,
    final_gain,
    cap_weight,
    cap_bias,
    image,
    modulation,
    w_qkv,
    w_out,
    w_cq,
    w_ckv,
    w_co,
):
    plane = lax.axis_size(PLANE)
    place = lax.axis_index(PLANE)
    prompts, tokens = token_ids.shape
    share = tokens // plane
    vocab_rows, feats = embed_table.shape
    units = wi_gate.shape[1]
    width = DT // plane

    local_ids = token_ids.reshape(-1) - place * vocab_rows
    one_hot = (local_ids[:, None] == jnp.arange(vocab_rows, dtype=jnp.int32)[None]).astype(BF16)
    picked = jnp.dot(one_hot, embed_table, preferred_element_type=F32).astype(BF16)
    picked = exchange(picked.reshape(plane, -1, feats), PLANE)

    pixels = image[0]
    rows = pixels.shape[0]
    modulate = modulation[0]
    modulated = call(modulate_kernel, "modulate", shape((rows, W)), (pixels, modulate))
    token_blocks = [modulated] + [shifted(modulated, "x", s) for s in range(1, 4)]
    weight_blocks = [w_qkv.T, crossed(w_qkv.T, "core", 1), crossed(w_qkv.T, "yhi", 1)]
    weight_blocks.append(crossed(weight_blocks[2], "core", 1))
    at = jnp.stack([lax.axis_index(a) for a in (SIDE, "x", "tp", PLANE)]).astype(jnp.int32)
    span = 4 * rows
    made = call(
        qkv_kernel,
        "query_key_value",
        [shape((3 * SLOT, span))] * 4 + [shape((2 * SLOT, span))] * 4,
        (at, *token_blocks, *weight_blocks),
        scratch=[pltpu.VMEM((span, W), BF16)],
        in_specs=[SMEM] + [VMEM] * 8,
        flops=2 * span * W * 12 * HEAD,
        moved=8 << 20,
        mib=56,
        tick=True,
    )
    fulls = [made[0]] + [crossed(made[m], SIDE, m) for m in range(1, 4)]
    others = [crossed(made[4 + m], SIDE + ("tp",), 2 * m + 1) for m in range(4)]

    def attend(first, after):
        found = call(
            attention_kernel,
            "self_attention",
            [shape((4, HEAD, rows))] * 2,
            (at, *(fulls[(first + s) % 4] for s in range(4)), *others),
            scratch=[
                pltpu.VMEM((2 * SLOT, 8 * span), BF16),
                pltpu.VMEM((8 * span, SLOT), BF16),
                pltpu.VMEM((8, ROWS, 2 * SLOT), BF16),
                pltpu.VMEM((ROWS, 8 * span), F32),
                pltpu.VMEM((ROWS, 8 * span), F32),
                pltpu.VMEM((8, HEAD, ROWS), BF16),
            ],
            in_specs=[SMEM] + [VMEM] * 8,
            flops=8 * span * 2 * span * 256 * 2,
            moved=8 << 20,
            exps=2 * span * 8 * span,
            after=after,
            tick=True,
            mib=56,
        )
        parts = [
            crossed(part, SIDE, first + m) if first + m else part
            for m, part in enumerate(found[:2])
        ]
        return parts, found[2:]

    embedded, tick = call(
        embed_kernel,
        "embed_sum",
        [shape(picked.shape)],
        (picked,),
        after=(tie(token_blocks[1], token_blocks[3], *weight_blocks[1:3]),),
        tick=True,
    )
    side = call(side_kernel, "side_weights", shape((w_out.shape[0], 3 * W)), (w_out, w_cq, w_co))
    pair = call(
        pair_kernel,
        "side_pair",
        shape((HEAD, 3 * W)),
        (at, side, crossed(side, "tp", 1)),
        in_specs=[SMEM, VMEM, VMEM],
        after=(tick,),
    )
    side = lax.all_gather(pair, SEQ, axis=0, tiled=True)
    gate_up = call(
        gate_up_kernel,
        "text_gate_up",
        shape((prompts, tokens + 2 * share, 2 * units)),
        (at, exchange(embedded, PLANE), ff_gain.reshape(1, feats), wi_gate.T, wi_up.T),
        scratch=[pltpu.VMEM((feats, 2 * units), BF16), pltpu.VMEM((tokens, feats), F32)],
        in_specs=[SMEM] + [VMEM] * 4,
        flops=4 * prompts * tokens * feats * units,
        moved=4 << 20,
        after=made[-1:],
    )
    down, tick = call(
        down_kernel,
        "text_down",
        [shape((plane, tokens + 2 * share, width))],
        (exchange(gate_up, "grp"), wo_down),
        flops=2 * tokens * DT * units,
        moved=5 << 20,
        exps=tokens * units,
        after=(tie(*fulls[1:], *others),),
        tick=True,
    )
    near, near_tick = attend(0, (tick,))
    cap_part, tick = call(
        cap_kernel,
        "caption_partial",
        [shape((plane, share, W + 128))],
        (exchange(down, PLANE), final_gain.reshape(1, width), cap_weight),
        scratch=[pltpu.VMEM((tokens, width), F32), pltpu.VMEM((tokens, W + 128), F32)],
        after=near_tick,
        tick=True,
    )
    far, far_tick = attend(2, (tick,))
    caption = call(
        caption_kernel,
        "caption",
        shape((plane, share, W)),
        (exchange(cap_part, PLANE), cap_bias.reshape(1, W)),
        after=far_tick,
    )
    *grouped, tick = call(
        regroup_kernel, "regroup", [shape((4, HEAD, rows))] * 4, (*near, *far), tick=True
    )
    parts = [grouped[0]] + [shifted(grouped[d], "x", d) for d in range(1, 4)]
    after_self, cross_query = project(at, parts, side, pixels, modulate[2:3])
    kv_part = call(
        kv_kernel,
        "text_kv",
        shape((plane, w_ckv.shape[1], tokens)),
        (exchange(caption, PLANE), w_ckv.T),
        scratch=[pltpu.VMEM((tokens, W), F32)],
        after=(tick,),
    )
    text_kv = exchange(kv_part, PLANE)
    result = cross(text_lengths, cross_query, after_self, text_kv, side)
    return result[None]


def solution(mesh):
    grp, seq, tp = mesh.devices.shape
    fine = Mesh(mesh.devices.reshape(grp, 2, seq // 4, 2, tp), ("grp",) + PLANE)
    placed = (
        P(),
        P("grp"),
        P(PLANE, "grp"),
        P("grp"),
        P("grp", PLANE),
        P("grp", PLANE),
        P(PLANE, None),
        P(PLANE),
        P(PLANE, None),
        P(),
        P("grp", PLANE, None),
        P("grp", None, None),
        P(None, SEQ),
        P(PLANE, None),
        P(PLANE, None),
        P(None, PLANE),
        P(PLANE, None),
    )
    return jax.shard_map(
        local, mesh=fine, in_specs=placed, out_specs=P("grp", PLANE, None), check_vma=False
    )
```

```python
import math

import jax
import jax.numpy as jnp
from jax import lax
from jax.experimental import pallas as pl
from jax.experimental.pallas import tpu as pltpu
from jax.sharding import Mesh
from jax.sharding import PartitionSpec as P

W = 1152
HEADS = 16
DT = 4096
HEAD = 72
SLOT = 80
LT = 128
EPSILON = 1e-06
PLANE = ("yhi", "x", "core", "tp")
SEQ = ("yhi", "x", "core")
SIDE = ("yhi", "core")
SCORE_SCALE = 1.0 / math.sqrt(HEAD)
EXP2_SCALE = SCORE_SCALE * math.log2(math.e)
LIFT = 64.0
F32 = jnp.float32
BF16 = jnp.bfloat16

VMEM = pl.BlockSpec(memory_space=pltpu.VMEM)
SMEM = pl.BlockSpec(memory_space=pltpu.SMEM)


def grant(mib):
    return pltpu.CompilerParams(vmem_limit_bytes=mib * 1024 * 1024)


def gelu_tanh(values):
    return jax.nn.gelu(values, approximate=True)


def exchange(blocks, axes):
    return lax.all_to_all(blocks, axes, 0, 0, tiled=True)


def shifted(value, axis, shift):
    size = lax.axis_size(axis)
    return lax.ppermute(value, axis, [(i, (i + shift) % size) for i in range(size)])


def crossed(value, axis, mask):
    size = lax.axis_size(axis)
    return lax.ppermute(value, axis, [(i, i ^ mask) for i in range(size)])


def nt_dot(a, b):
    return lax.dot_general(a, b, (((1,), (1,)), ((), ())), preferred_element_type=F32)


def thirds(values):
    high = values.astype(BF16).astype(F32)
    mid = (values - high).astype(BF16).astype(F32)
    return high, mid, values - high - mid


TICK = (8, 128)


def call(
    kernel,
    name,
    out_shape,
    args,
    scratch=(),
    in_specs=None,
    flops=0,
    moved=1 << 20,
    exps=0,
    after=(),
    tick=False,
    mib=16,
):
    outs = list(out_shape) if isinstance(out_shape, list) else [out_shape]
    many = tick or isinstance(out_shape, list)
    if tick:
        outs.append(shape(TICK, F32))
    first, waits = len(args), len(after)
    last = first + waits + len(outs)

    def body(*refs):
        if tick:
            refs[last - 1][...] = jnp.zeros(TICK, F32)
        kernel(*refs[:first], *refs[first + waits : last - tick], *refs[last:])

    return pl.pallas_call(
        body,
        out_shape=outs if many else outs[0],
        in_specs=(in_specs or [VMEM] * len(args)) + [VMEM] * waits,
        out_specs=[VMEM] * len(outs) if many else VMEM,
        scratch_shapes=list(scratch),
        compiler_params=grant(mib),
        cost_estimate=pl.CostEstimate(flops=flops, bytes_accessed=moved, transcendentals=exps),
        name=name,
    )(*args, *after)


def tie(*arrays):
    total = jnp.zeros(TICK, F32)
    for array in arrays:
        total = total + array[: TICK[0], : TICK[1]].astype(F32)
    return total


def shape(dims, dtype=BF16):
    return jax.ShapeDtypeStruct(dims, dtype)


def embed_kernel(in_ref, out_ref):
    total = in_ref[0].astype(F32)
    for j in range(1, in_ref.shape[0]):
        total += in_ref[j].astype(F32)
    total = total.astype(BF16)
    for j in range(out_ref.shape[0]):
        out_ref[j] = total


def row_of(column):
    return jnp.broadcast_to(column, (column.shape[0], 128)).T[:1]


def column_of(row):
    return jnp.broadcast_to(row, (128, row.shape[1])).T[:, :1]


def gate_up_kernel(at_ref, in_ref, gain_ref, gate_ref, up_ref, out_ref, weight, rows32):
    prompts, _, both = out_ref.shape
    plane, group, feats = in_ref.shape
    tokens = plane * group // prompts
    share = tokens // plane
    weight[...] = (
        jnp.concatenate([gate_ref[...].astype(F32), up_ref[...].astype(F32)], axis=0)
        .T.astype(BF16)
    )
    per = plane // prompts
    at = at_ref[3] * share
    base = pl.multiple_of(at // 8 * 8, 8)
    upper = lax.rem(at, 8) == 0
    for p in range(prompts):
        rows = in_ref[p * per : (p + 1) * per].reshape(tokens, feats).astype(F32)
        rows32[...] = rows
        scaled = (rows * gain_ref[...]).astype(BF16)
        out_ref[p, :tokens, :] = jnp.dot(
            scaled, weight[...], preferred_element_type=F32
        ).astype(BF16)
        near = rows32[pl.ds(base, 8), :]
        own = jnp.where(upper, near[:share], near[share:])
        square = row_of(jnp.sum(rows * rows, axis=-1, keepdims=True))
        squares = jnp.concatenate(list(thirds(square)) + [jnp.zeros_like(square)], axis=0)
        out_ref[p, tokens:, :] = jnp.concatenate(
            [
                jnp.concatenate([own, jnp.zeros((share, both - feats), F32)], axis=1),
                jnp.concatenate([squares, jnp.zeros((4, both - tokens), F32)], axis=1),
            ],
            axis=0,
        ).astype(BF16)


def down_kernel(in_ref, down_ref, out_ref):
    groups, rows, both = in_ref.shape
    plane, _, width = out_ref.shape
    tokens = 128
    share = tokens // plane
    units = down_ref.shape[0]
    feats = DT // groups
    total = in_ref[0, :tokens, :].astype(F32)
    square = None
    for g in range(groups):
        if g:
            total += in_ref[g, :tokens, :].astype(F32)
        extra = in_ref[g, tokens:, :].astype(F32)
        for i in range(3):
            part = extra[share + i : share + i + 1, :tokens]
            square = part if square is None else square + part
        for k in range(feats // width):
            piece = extra[:share, k * width : (k + 1) * width]
            out_ref[g * (feats // width) + k, tokens:, :] = jnp.concatenate(
                [piece, jnp.zeros_like(piece)], axis=0
            ).astype(BF16)
    inverse = column_of(lax.rsqrt(square / DT + EPSILON))
    total = total * inverse
    hidden = (gelu_tanh(total[:, :units]) * total[:, units:]).astype(BF16)
    step = 4
    for j in range(0, plane, step):
        part = jnp.dot(
            hidden, down_ref[:, j * width : (j + step) * width], preferred_element_type=F32
        ).astype(BF16)
        for k in range(step):
            out_ref[j + k, :tokens, :] = part[:, k * width : (k + 1) * width]


def cap_kernel(in_ref, gain_ref, weight_ref, out_ref, rest, wide):
    plane, share, _ = out_ref.shape
    tokens = plane * share
    total = in_ref[0, :tokens, :].astype(F32)
    for j in range(1, plane):
        total += in_ref[j, :tokens, :].astype(F32)
    for j in range(plane):
        rest[j * share : (j + 1) * share, :] = in_ref[j, tokens:, :].astype(F32)[:share]
    state = total + rest[...]
    high, mid, low = thirds(jnp.sum(state * state, axis=-1, keepdims=True))
    lane = lax.broadcasted_iota(jnp.int32, (tokens, wide.shape[1] - W), 1)
    wide[:, W:] = jnp.where(
        lane == 0, high, jnp.where(lane == 1, mid, jnp.where(lane == 2, low, 0.0))
    )
    gained = (state * gain_ref[...]).astype(BF16)
    wide[:, :W] = jnp.dot(gained, weight_ref[...], preferred_element_type=F32)
    for j in range(plane):
        out_ref[j] = wide[j * share : (j + 1) * share, :].astype(BF16)


def caption_kernel(in_ref, bias_ref, out_ref):
    total = in_ref[0].astype(F32)
    for j in range(1, in_ref.shape[0]):
        total += in_ref[j].astype(F32)
    square = total[:, W : W + 1] + total[:, W + 1 : W + 2] + total[:, W + 2 : W + 3]
    inverse = lax.rsqrt(square / DT + EPSILON)
    caption = gelu_tanh(total[:, :W] * inverse + bias_ref[...]).astype(BF16)
    for j in range(out_ref.shape[0]):
        out_ref[j] = caption


def kv_kernel(in_ref, weight_ref, out_ref, rows):
    plane, share, _ = in_ref.shape
    for j in range(plane):
        rows[j * share : (j + 1) * share, :] = in_ref[j].astype(F32)
    kv = nt_dot(weight_ref[...], rows[...].astype(BF16)).astype(BF16)
    for j in range(plane):
        out_ref[j] = kv


def modulate_kernel(image_ref, mod_ref, out_ref):
    pixels = image_ref[...].astype(F32)
    center = jnp.mean(pixels, axis=-1, keepdims=True)
    spread = jnp.mean((pixels - center) ** 2, axis=-1, keepdims=True)
    out_ref[...] = (
        (pixels - center) * lax.rsqrt(spread + EPSILON) * (1.0 + mod_ref[1:2]) + mod_ref[0:1]
    ).astype(BF16)


def side_kernel(*refs):
    out_ref = refs[-1]
    for k, ref in enumerate(refs[:-1]):
        out_ref[:, k * W : (k + 1) * W] = ref[...]


def pair_kernel(at_ref, own_ref, other_ref, out_ref):
    own, other = own_ref[...].astype(F32), other_ref[...].astype(F32)
    first = at_ref[2] == 0
    out_ref[...] = jnp.concatenate(
        [jnp.where(first, own, other), jnp.where(first, other, own)], axis=0
    ).astype(BF16)


def qkv_kernel(at_ref, *refs):
    tokens, weights = refs[:4], refs[4:8]
    fulls, pairs = refs[8:12], refs[12:16]
    x_rows = refs[16]
    rows = tokens[0].shape[0]
    for m, block in enumerate(tokens):
        at = lax.rem(at_ref[1] - m + 4, 4)
        x_rows[pl.ds(pl.multiple_of(at * rows, rows), rows), :] = block[...]
    span = x_rows.shape[0]
    zeros = jnp.zeros((SLOT - HEAD, span), F32)
    ones = (lax.broadcasted_iota(jnp.int32, zeros.shape, 0) == 0).astype(F32)
    for s in range(4):
        out = nt_dot(weights[s][...], x_rows[...])
        slots = [
            jnp.concatenate([out[i * HEAD : (i + 1) * HEAD], tail], axis=0).astype(BF16)
            for i, tail in enumerate((zeros, ones, zeros))
        ]
        for i in range(3):
            fulls[s][i * SLOT : (i + 1) * SLOT, :] = slots[i]
        for i in range(2):
            pairs[s][i * SLOT : (i + 1) * SLOT, :] = slots[i + 1]


ROWS = 192
TILE = 256


def attention_kernel(at_ref, *refs):
    fulls, others = refs[:4], refs[4:8]
    outs = refs[8:12]
    keys, vals, qry, terms_a, terms_b, found = refs[12:18]
    span = fulls[0].shape[1]
    count = 8 * span
    largest = None
    for c, (ref, first) in enumerate([(r, SLOT) for r in fulls] + [(r, 0) for r in others]):
        block = ref[first : first + SLOT, :]
        cols = slice(c * span, (c + 1) * span)
        keys[:SLOT, cols] = block
        keys[SLOT:, cols] = block
        vals[cols, :] = ref[first + SLOT : first + 2 * SLOT, :].astype(F32).T.astype(BF16)
        wide = block.astype(F32)
        row = lax.broadcasted_iota(jnp.int32, wide.shape, 0)
        norm = jnp.sum(jnp.where(row < HEAD, wide * wide, 0.0), axis=0, keepdims=True)
        largest = norm if largest is None else jnp.maximum(largest, norm)
    largest = jnp.max(largest, axis=-1, keepdims=True)
    for s in range(4):
        q = fulls[s][0:SLOT, :].astype(F32) * SCORE_SCALE
        high = q.astype(BF16).astype(F32)
        row = lax.broadcasted_iota(jnp.int32, q.shape, 0)
        bound = jnp.sqrt(jnp.sum(q * q, axis=0, keepdims=True) * largest) * (1.0 + 2.0**-6)
        high = jnp.where(row == HEAD, LIFT * math.log(2.0) - bound, high)
        low = jnp.where(row == HEAD, 0.0, q - high)
        both = jnp.concatenate([high, low], axis=0).T
        for a in range(4):
            away = lax.rem(a - at_ref[1] + 4, 4)
            qry[s * 4 + away] = both[a * ROWS : (a + 1) * ROWS].astype(BF16)

    def tile(t):
        return slice(t * TILE, (t + 1) * TILE)

    def fill(q, t, terms, total, shift=None):
        s = jnp.dot(q, keys[:, tile(t)], preferred_element_type=F32)
        e = jnp.exp(s if shift is None else s - shift)
        terms[:, tile(t)] = e
        return total + (e[:, :128] + e[:, 128:])

    def weigh(t, terms, inverse, acc):
        p = (terms[:, tile(t)] * inverse).astype(BF16)
        return acc + jnp.dot(p, vals[tile(t), :], preferred_element_type=F32)

    def put(i, acc):
        found[i] = acc.T[:HEAD].astype(BF16)

    tiles = count // TILE
    none = jnp.zeros((ROWS, 128), F32)
    empty = jnp.zeros((ROWS, SLOT), F32)

    def step(i, seen):
        one, two = qry[2 * i], qry[2 * i + 1]
        total_a, total_b, acc_a, acc_b = none, none, empty, empty
        for t in range(tiles):
            total_a = fill(one, t, terms_a, total_a)
        total_a = jnp.sum(total_a, axis=-1, keepdims=True)
        inverse = 1.0 / total_a
        for t in range(tiles):
            total_b = fill(two, t, terms_b, total_b)
            acc_a = weigh(t, terms_a, inverse, acc_a)
        put(2 * i, acc_a)
        total_b = jnp.sum(total_b, axis=-1, keepdims=True)
        inverse = 1.0 / total_b
        for t in range(tiles):
            acc_b = weigh(t, terms_b, inverse, acc_b)
        put(2 * i + 1, acc_b)
        least, most = seen
        return (
            jnp.minimum(least, jnp.min(jnp.minimum(total_a, total_b))),
            jnp.maximum(most, jnp.max(jnp.maximum(total_a, total_b))),
        )

    least, most = lax.fori_loop(0, 8, step, (jnp.float32(1.0), jnp.float32(1.0)))
    safe = jnp.logical_and(least > 2.0**-76, most < 2.0**100)

    @pl.when(jnp.logical_not(safe))
    def _():
        def again(i, _):
            q = qry[i].astype(F32)
            lane = lax.broadcasted_iota(jnp.int32, q.shape, 1)
            q = jnp.where(lane == HEAD, 0.0, q).astype(BF16)
            top = None
            for t in range(tiles):
                s = jnp.dot(q, keys[:, tile(t)], preferred_element_type=F32)
                here = jnp.max(s, axis=-1, keepdims=True)
                top = here if top is None else jnp.maximum(top, here)
            total = none
            for t in range(tiles):
                total = fill(q, t, terms_a, total, top)
            inverse = 1.0 / jnp.sum(total, axis=-1, keepdims=True)
            acc = empty
            for t in range(tiles):
                acc = weigh(t, terms_a, inverse, acc)
            put(i, acc)
            return 0

        lax.fori_loop(0, 16, again, 0)

    for s, out in enumerate(outs):
        out[...] = found[4 * s : 4 * s + 4]


def regroup_kernel(*refs):
    for m, out in enumerate(refs[4:]):
        for s, part in enumerate(refs[:4]):
            out[s] = part[m]


def project_kernel(at_ref, *refs):
    parts = refs[:4]
    wout_ref, wcq_ref, img_ref, gate_ref, after_ref, cq_ref, wide = refs[4:]
    for d, part in enumerate(parts):
        x = lax.rem(at_ref[1] - d + 4, 4)
        for m in range(4):
            side = lax.bitwise_xor(at_ref[0], m)
            head = (side // 2) * 8 + x * 2 + lax.rem(side, 2)
            wide[pl.ds(pl.multiple_of(head * HEAD, 8), HEAD), :] = part[m].astype(F32)
    projected = jnp.dot(wide[...].T.astype(BF16), wout_ref[...], preferred_element_type=F32)
    after = (img_ref[...].astype(F32) + gate_ref[...] * projected).astype(BF16)
    after_ref[...] = after
    cq_ref[...] = jnp.dot(after, wcq_ref[...], preferred_element_type=F32).astype(BF16)


def cross_kernel(len_ref, cq_ref, after_ref, kv_ref, wco_ref, out_ref, wide):
    length = len_ref[0]
    rows = cq_ref.shape[0]
    visible = lax.broadcasted_iota(jnp.int32, (rows, LT), 1) < length
    for h in range(HEADS):
        qry = cq_ref[:, h * HEAD : (h + 1) * HEAD]
        s = jnp.dot(qry, kv_ref[h], preferred_element_type=F32) * SCORE_SCALE
        s = jnp.where(visible, s, -1e30)
        e = jnp.exp(s - jnp.max(s, axis=-1, keepdims=True))
        p = (e / jnp.sum(e, axis=-1, keepdims=True)).astype(BF16)
        wide[h * HEAD : (h + 1) * HEAD, :] = nt_dot(kv_ref[HEADS + h], p)
    final = jnp.dot(wide[...].T.astype(BF16), wco_ref[...], preferred_element_type=F32)
    out_ref[...] = (after_ref[...].astype(F32) + final).astype(BF16)


def whole(dims):
    return pl.BlockSpec(dims, lambda i: (0,) * len(dims))


def third(k):
    return pl.BlockSpec((W, W), lambda i: (0, k))


def project(at, parts, side, img, gate):
    rows = img.shape[0]
    return pl.pallas_call(
        project_kernel,
        grid=(1,),
        out_shape=[shape((rows, W))] * 2,
        in_specs=[SMEM]
        + [whole(part.shape) for part in parts]
        + [third(0), third(1), whole(img.shape), whole(gate.shape)],
        out_specs=[whole((rows, W))] * 2,
        scratch_shapes=[pltpu.VMEM((W, rows), F32)],
        compiler_params=grant(56),
        cost_estimate=pl.CostEstimate(
            flops=4 * rows * W * W, bytes_accessed=8 << 20, transcendentals=0
        ),
        name="project_out_and_query",
    )(at, *parts, side, side, img, gate)


def cross(length, cq, after, kv, side):
    rows = cq.shape[0]
    return pl.pallas_call(
        cross_kernel,
        grid=(1,),
        out_shape=shape((rows, W)),
        in_specs=[SMEM, whole(cq.shape), whole(after.shape), whole(kv.shape), third(2)],
        out_specs=whole((rows, W)),
        scratch_shapes=[pltpu.VMEM((W, rows), F32)],
        compiler_params=grant(56),
        cost_estimate=pl.CostEstimate(
            flops=4 * rows * W * W, bytes_accessed=5 << 20, transcendentals=rows * LT * HEADS
        ),
        name="cross_attention",
    )(length, cq, after, kv, side)


def local(
    token_ids,
    text_lengths,
    embed_table,
    ff_gain,
    wi_gate,
    wi_up,
    wo_down,
    final_gain,
    cap_weight,
    cap_bias,
    image,
    modulation,
    w_qkv,
    w_out,
    w_cq,
    w_ckv,
    w_co,
):
    plane = lax.axis_size(PLANE)
    place = lax.axis_index(PLANE)
    prompts, tokens = token_ids.shape
    share = tokens // plane
    vocab_rows, feats = embed_table.shape
    units = wi_gate.shape[1]
    width = DT // plane

    local_ids = token_ids.reshape(-1) - place * vocab_rows
    one_hot = (local_ids[:, None] == jnp.arange(vocab_rows, dtype=jnp.int32)[None]).astype(BF16)
    picked = jnp.dot(one_hot, embed_table, preferred_element_type=F32).astype(BF16)
    picked = exchange(picked.reshape(plane, -1, feats), PLANE)

    pixels = image[0]
    rows = pixels.shape[0]
    modulate = modulation[0]
    modulated = call(modulate_kernel, "modulate", shape((rows, W)), (pixels, modulate))
    token_blocks = [modulated] + [shifted(modulated, "x", s) for s in range(1, 4)]
    weight_blocks = [w_qkv.T, crossed(w_qkv.T, "core", 1), crossed(w_qkv.T, "yhi", 1)]
    weight_blocks.append(crossed(weight_blocks[2], "core", 1))
    at = jnp.stack([lax.axis_index(a) for a in (SIDE, "x", "tp", PLANE)]).astype(jnp.int32)
    span = 4 * rows
    made = call(
        qkv_kernel,
        "query_key_value",
        [shape((3 * SLOT, span))] * 4 + [shape((2 * SLOT, span))] * 4,
        (at, *token_blocks, *weight_blocks),
        scratch=[pltpu.VMEM((span, W), BF16)],
        in_specs=[SMEM] + [VMEM] * 8,
        flops=2 * span * W * 12 * HEAD,
        moved=8 << 20,
        mib=56,
        tick=True,
    )
    fulls = [made[0]] + [crossed(made[m], SIDE, m) for m in range(1, 4)]
    others = [crossed(made[4 + m], SIDE + ("tp",), 2 * m + 1) for m in range(4)]

    embedded = call(
        embed_kernel,
        "embed_sum",
        shape(picked.shape),
        (picked,),
        after=(tie(*token_blocks[1:], *weight_blocks[1:]),),
    )
    gate_up, tick = call(
        gate_up_kernel,
        "text_gate_up",
        [shape((prompts, tokens + 2 * share, 2 * units))],
        (at, exchange(embedded, PLANE), ff_gain.reshape(1, feats), wi_gate.T, wi_up.T),
        scratch=[pltpu.VMEM((feats, 2 * units), BF16), pltpu.VMEM((tokens, feats), F32)],
        in_specs=[SMEM] + [VMEM] * 4,
        flops=4 * prompts * tokens * feats * units,
        moved=4 << 20,
        after=(tie(*fulls[1:], *others),),
        tick=True,
    )
    side = call(side_kernel, "side_weights", shape((w_out.shape[0], 3 * W)), (w_out, w_cq, w_co))
    pair = call(
        pair_kernel,
        "side_pair",
        shape((HEAD, 3 * W)),
        (at, side, crossed(side, "tp", 1)),
        in_specs=[SMEM, VMEM, VMEM],
        after=(tick,),
    )
    side = lax.all_gather(pair, SEQ, axis=0, tiled=True)
    *found, attended = call(
        attention_kernel,
        "self_attention",
        [shape((4, HEAD, rows))] * 4,
        (at, *fulls, *others),
        scratch=[
            pltpu.VMEM((2 * SLOT, 8 * span), BF16),
            pltpu.VMEM((8 * span, SLOT), BF16),
            pltpu.VMEM((16, ROWS, 2 * SLOT), BF16),
            pltpu.VMEM((ROWS, 8 * span), F32),
            pltpu.VMEM((ROWS, 8 * span), F32),
            pltpu.VMEM((16, HEAD, ROWS), BF16),
        ],
        in_specs=[SMEM] + [VMEM] * 8,
        flops=16 * span * 2 * span * 256 * 2,
        moved=8 << 20,
        exps=4 * span * 8 * span,
        after=(tick,),
        tick=True,
        mib=56,
    )
    found = [found[0]] + [crossed(found[m], SIDE, m) for m in range(1, 4)]
    down = call(
        down_kernel,
        "text_down",
        shape((plane, tokens + 2 * share, width)),
        (exchange(gate_up, "grp"), wo_down),
        flops=2 * tokens * DT * units,
        moved=5 << 20,
        exps=tokens * units,
        after=(attended,),
    )
    cap_part = call(
        cap_kernel,
        "caption_partial",
        shape((plane, share, W + 128)),
        (exchange(down, PLANE), final_gain.reshape(1, width), cap_weight),
        scratch=[pltpu.VMEM((tokens, width), F32), pltpu.VMEM((tokens, W + 128), F32)],
    )
    *grouped, tick = call(
        regroup_kernel, "regroup", [shape((4, HEAD, rows))] * 4, tuple(found), tick=True
    )
    caption = call(
        caption_kernel,
        "caption",
        shape((plane, share, W)),
        (exchange(cap_part, PLANE), cap_bias.reshape(1, W)),
        after=(tick,),
    )
    parts = [grouped[0]] + [shifted(grouped[d], "x", d) for d in range(1, 4)]
    after_self, cross_query = project(at, parts, side, pixels, modulate[2:3])
    kv_part = call(
        kv_kernel,
        "text_kv",
        shape((plane, w_ckv.shape[1], tokens)),
        (exchange(caption, PLANE), w_ckv.T),
        scratch=[pltpu.VMEM((tokens, W), F32)],
        after=(tie(*(part[0] for part in parts[1:])),),
    )
    text_kv = exchange(kv_part, PLANE)
    result = cross(text_lengths, cross_query, after_self, text_kv, side)
    return result[None]


def solution(mesh):
    grp, seq, tp = mesh.devices.shape
    fine = Mesh(mesh.devices.reshape(grp, 2, seq // 4, 2, tp), ("grp",) + PLANE)
    placed = (
        P(),
        P("grp"),
        P(PLANE, "grp"),
        P("grp"),
        P("grp", PLANE),
        P("grp", PLANE),
        P(PLANE, None),
        P(PLANE),
        P(PLANE, None),
        P(),
        P("grp", PLANE, None),
        P("grp", None, None),
        P(None, SEQ),
        P(PLANE, None),
        P(PLANE, None),
        P(None, PLANE),
        P(PLANE, None),
    )
    return jax.shard_map(
        local, mesh=fine, in_specs=placed, out_specs=P("grp", PLANE, None), check_vma=False
    )
```

```python
import math

import jax
import jax.numpy as jnp
from jax import lax
from jax.experimental import pallas as pl
from jax.experimental.pallas import tpu as pltpu
from jax.sharding import Mesh
from jax.sharding import PartitionSpec as P

W = 1152
HEADS = 16
DT = 4096
HEAD = 72
SLOT = 80
LT = 128
EPSILON = 1e-06
PLANE = ("yhi", "x", "core", "tp")
SEQ = ("yhi", "x", "core")
SIDE = ("yhi", "core")
ROW = ("yhi", "tp")
SCORE_SCALE = 1.0 / math.sqrt(HEAD)
EXP2_SCALE = SCORE_SCALE * math.log2(math.e)
LIFT = 64.0
F32 = jnp.float32
BF16 = jnp.bfloat16

VMEM = pl.BlockSpec(memory_space=pltpu.VMEM)
SMEM = pl.BlockSpec(memory_space=pltpu.SMEM)


def grant(mib):
    return pltpu.CompilerParams(vmem_limit_bytes=mib * 1024 * 1024)


def gelu_tanh(values):
    return jax.nn.gelu(values, approximate=True)


def exchange(blocks, axes):
    return lax.all_to_all(blocks, axes, 0, 0, tiled=True)


def shifted(value, axis, shift):
    size = lax.axis_size(axis)
    return lax.ppermute(value, axis, [(i, (i + shift) % size) for i in range(size)])


def crossed(value, axis, mask):
    size = lax.axis_size(axis)
    return lax.ppermute(value, axis, [(i, i ^ mask) for i in range(size)])


def nt_dot(a, b):
    return lax.dot_general(a, b, (((1,), (1,)), ((), ())), preferred_element_type=F32)


def thirds(values):
    high = values.astype(BF16).astype(F32)
    mid = (values - high).astype(BF16).astype(F32)
    return high, mid, values - high - mid


TICK = (8, 128)


def call(
    kernel,
    name,
    out_shape,
    args,
    scratch=(),
    in_specs=None,
    flops=0,
    moved=1 << 20,
    exps=0,
    after=(),
    tick=False,
    mib=16,
):
    outs = list(out_shape) if isinstance(out_shape, list) else [out_shape]
    many = tick or isinstance(out_shape, list)
    if tick:
        outs.append(shape(TICK, F32))
    first, waits = len(args), len(after)
    last = first + waits + len(outs)

    def body(*refs):
        if tick:
            refs[last - 1][...] = jnp.zeros(TICK, F32)
        kernel(*refs[:first], *refs[first + waits : last - tick], *refs[last:])

    return pl.pallas_call(
        body,
        out_shape=outs if many else outs[0],
        in_specs=(in_specs or [VMEM] * len(args)) + [VMEM] * waits,
        out_specs=[VMEM] * len(outs) if many else VMEM,
        scratch_shapes=list(scratch),
        compiler_params=grant(mib),
        cost_estimate=pl.CostEstimate(flops=flops, bytes_accessed=moved, transcendentals=exps),
        name=name,
    )(*args, *after)


def tie(*arrays):
    total = jnp.zeros(TICK, F32)
    for array in arrays:
        total = total + array[: TICK[0], : TICK[1]].astype(F32)
    return total


def shape(dims, dtype=BF16):
    return jax.ShapeDtypeStruct(dims, dtype)


def embed_kernel(in_ref, out_ref):
    total = in_ref[0].astype(F32)
    for j in range(1, in_ref.shape[0]):
        total += in_ref[j].astype(F32)
    total = total.astype(BF16)
    for j in range(out_ref.shape[0]):
        out_ref[j] = total


def row_of(column):
    return jnp.broadcast_to(column, (column.shape[0], 128)).T[:1]


def column_of(row):
    return jnp.broadcast_to(row, (128, row.shape[1])).T[:, :1]


def gate_up_kernel(at_ref, in_ref, gain_ref, gate_ref, up_ref, out_ref, weight, rows32):
    prompts, _, both = out_ref.shape
    plane, group, feats = in_ref.shape
    tokens = plane * group // prompts
    share = tokens // plane
    weight[...] = (
        jnp.concatenate([gate_ref[...].astype(F32), up_ref[...].astype(F32)], axis=0)
        .T.astype(BF16)
    )
    per = plane // prompts
    at = at_ref[3] * share
    base = pl.multiple_of(at // 8 * 8, 8)
    upper = lax.rem(at, 8) == 0
    for p in range(prompts):
        rows = in_ref[p * per : (p + 1) * per].reshape(tokens, feats).astype(F32)
        rows32[...] = rows
        scaled = (rows * gain_ref[...]).astype(BF16)
        out_ref[p, :tokens, :] = jnp.dot(
            scaled, weight[...], preferred_element_type=F32
        ).astype(BF16)
        near = rows32[pl.ds(base, 8), :]
        own = jnp.where(upper, near[:share], near[share:])
        square = row_of(jnp.sum(rows * rows, axis=-1, keepdims=True))
        squares = jnp.concatenate(list(thirds(square)) + [jnp.zeros_like(square)], axis=0)
        out_ref[p, tokens:, :] = jnp.concatenate(
            [
                jnp.concatenate([own, jnp.zeros((share, both - feats), F32)], axis=1),
                jnp.concatenate([squares, jnp.zeros((4, both - tokens), F32)], axis=1),
            ],
            axis=0,
        ).astype(BF16)


def down_kernel(in_ref, down_ref, out_ref):
    groups, rows, both = in_ref.shape
    plane, _, width = out_ref.shape
    tokens = 128
    share = tokens // plane
    units = down_ref.shape[0]
    feats = DT // groups
    total = in_ref[0, :tokens, :].astype(F32)
    square = None
    for g in range(groups):
        if g:
            total += in_ref[g, :tokens, :].astype(F32)
        extra = in_ref[g, tokens:, :].astype(F32)
        for i in range(3):
            part = extra[share + i : share + i + 1, :tokens]
            square = part if square is None else square + part
        for k in range(feats // width):
            piece = extra[:share, k * width : (k + 1) * width]
            out_ref[g * (feats // width) + k, tokens:, :] = jnp.concatenate(
                [piece, jnp.zeros_like(piece)], axis=0
            ).astype(BF16)
    inverse = column_of(lax.rsqrt(square / DT + EPSILON))
    total = total * inverse
    hidden = (gelu_tanh(total[:, :units]) * total[:, units:]).astype(BF16)
    step = 4
    for j in range(0, plane, step):
        part = jnp.dot(
            hidden, down_ref[:, j * width : (j + step) * width], preferred_element_type=F32
        ).astype(BF16)
        for k in range(step):
            out_ref[j + k, :tokens, :] = part[:, k * width : (k + 1) * width]


def cap_kernel(in_ref, gain_ref, weight_ref, out_ref, rest, wide):
    plane, share, _ = out_ref.shape
    tokens = plane * share
    total = in_ref[0, :tokens, :].astype(F32)
    for j in range(1, plane):
        total += in_ref[j, :tokens, :].astype(F32)
    for j in range(plane):
        rest[j * share : (j + 1) * share, :] = in_ref[j, tokens:, :].astype(F32)[:share]
    state = total + rest[...]
    high, mid, low = thirds(jnp.sum(state * state, axis=-1, keepdims=True))
    lane = lax.broadcasted_iota(jnp.int32, (tokens, wide.shape[1] - W), 1)
    wide[:, W:] = jnp.where(
        lane == 0, high, jnp.where(lane == 1, mid, jnp.where(lane == 2, low, 0.0))
    )
    gained = (state * gain_ref[...]).astype(BF16)
    wide[:, :W] = jnp.dot(gained, weight_ref[...], preferred_element_type=F32)
    for j in range(plane):
        out_ref[j] = wide[j * share : (j + 1) * share, :].astype(BF16)


def caption_kernel(in_ref, bias_ref, out_ref):
    total = in_ref[0].astype(F32)
    for j in range(1, in_ref.shape[0]):
        total += in_ref[j].astype(F32)
    square = total[:, W : W + 1] + total[:, W + 1 : W + 2] + total[:, W + 2 : W + 3]
    inverse = lax.rsqrt(square / DT + EPSILON)
    caption = gelu_tanh(total[:, :W] * inverse + bias_ref[...]).astype(BF16)
    for j in range(out_ref.shape[0]):
        out_ref[j] = caption


def kv_kernel(in_ref, weight_ref, out_ref, rows):
    plane, share, _ = in_ref.shape
    for j in range(plane):
        rows[j * share : (j + 1) * share, :] = in_ref[j].astype(F32)
    kv = nt_dot(weight_ref[...], rows[...].astype(BF16)).astype(BF16)
    for j in range(plane):
        out_ref[j] = kv


def modulate_kernel(image_ref, mod_ref, weight_ref, out_ref, copy_ref):
    copy_ref[...] = weight_ref[...]
    pixels = image_ref[...].astype(F32)
    center = jnp.mean(pixels, axis=-1, keepdims=True)
    spread = jnp.mean((pixels - center) ** 2, axis=-1, keepdims=True)
    out_ref[...] = (
        (pixels - center) * lax.rsqrt(spread + EPSILON) * (1.0 + mod_ref[1:2]) + mod_ref[0:1]
    ).astype(BF16)


def side_kernel(*refs):
    out_ref = refs[-1]
    for k, ref in enumerate(refs[:-1]):
        out_ref[:, k * W : (k + 1) * W] = ref[...]


def pair_kernel(at_ref, own_ref, other_ref, out_ref):
    own, other = own_ref[...].astype(F32), other_ref[...].astype(F32)
    first = at_ref[2] == 0
    out_ref[...] = jnp.concatenate(
        [jnp.where(first, own, other), jnp.where(first, other, own)], axis=0
    ).astype(BF16)


def qkv_kernel(at_ref, *refs):
    tokens, weights = refs[:4], refs[4:8]
    fulls = refs[8:12]
    x_rows, by_chip = refs[12:14]
    rows = tokens[0].shape[0]
    for m, block in enumerate(tokens):
        at = lax.rem(at_ref[1] - m + 4, 4)
        x_rows[pl.ds(pl.multiple_of(at * rows, rows), rows), :] = block[...]
    for m, block in enumerate(weights):
        by_chip[lax.bitwise_xor(at_ref[4], m)] = block[...]
    span = x_rows.shape[0]
    zeros = jnp.zeros((SLOT - HEAD, span), F32)
    ones = (lax.broadcasted_iota(jnp.int32, zeros.shape, 0) == 0).astype(F32)
    for s in range(4):
        out = nt_dot(by_chip[s], x_rows[...])
        for i, tail in enumerate((zeros, ones, zeros)):
            fulls[s][i * SLOT : (i + 1) * SLOT, :] = jnp.concatenate(
                [out[i * HEAD : (i + 1) * HEAD], tail], axis=0
            ).astype(BF16)


ROWS = 192
TILE = 256


def attention_kernel(at_ref, *refs):
    fulls, others = refs[:4], refs[4:8]
    outs = refs[8:12]
    keys, vals, qry, terms_a, terms_b, found = refs[12:18]
    span = fulls[0].shape[1]
    count = 8 * span
    largest = None
    for c, ref in enumerate(fulls + others):
        block = ref[SLOT : 2 * SLOT, :]
        cols = slice(c * span, (c + 1) * span)
        keys[:SLOT, cols] = block
        keys[SLOT:, cols] = block
        vals[cols, :] = ref[2 * SLOT : 3 * SLOT, :].astype(F32).T.astype(BF16)
        wide = block.astype(F32)
        row = lax.broadcasted_iota(jnp.int32, wide.shape, 0)
        norm = jnp.sum(jnp.where(row < HEAD, wide * wide, 0.0), axis=0, keepdims=True)
        largest = norm if largest is None else jnp.maximum(largest, norm)
    largest = jnp.max(largest, axis=-1, keepdims=True)
    for s in range(4):
        q = fulls[s][0:SLOT, :].astype(F32) * SCORE_SCALE
        high = q.astype(BF16).astype(F32)
        row = lax.broadcasted_iota(jnp.int32, q.shape, 0)
        bound = jnp.sqrt(jnp.sum(q * q, axis=0, keepdims=True) * largest) * (1.0 + 2.0**-6)
        high = jnp.where(row == HEAD, LIFT * math.log(2.0) - bound, high)
        low = jnp.where(row == HEAD, 0.0, q - high)
        both = jnp.concatenate([high, low], axis=0).T
        for a in range(4):
            away = lax.rem(a - at_ref[1] + 4, 4)
            qry[s * 4 + away] = both[a * ROWS : (a + 1) * ROWS].astype(BF16)

    def tile(t):
        return slice(t * TILE, (t + 1) * TILE)

    def fill(q, t, terms, total, shift=None):
        s = jnp.dot(q, keys[:, tile(t)], preferred_element_type=F32)
        e = jnp.exp(s if shift is None else s - shift)
        terms[:, tile(t)] = e
        return total + (e[:, :128] + e[:, 128:])

    def weigh(t, terms, inverse, acc):
        p = (terms[:, tile(t)] * inverse).astype(BF16)
        return acc + jnp.dot(p, vals[tile(t), :], preferred_element_type=F32)

    def put(i, acc):
        found[i] = acc.T[:HEAD].astype(BF16)

    tiles = count // TILE
    none = jnp.zeros((ROWS, 128), F32)
    empty = jnp.zeros((ROWS, SLOT), F32)

    def sums(total):
        total = jnp.sum(total, axis=-1, keepdims=True)
        return total, 1.0 / total

    blocks = qry.shape[0]
    terms_b[...] = jnp.zeros(terms_b.shape, F32)

    def step(i, carry):
        inverse_b, least, most = carry
        one, two = qry[2 * i], qry[2 * i + 1]
        total_a, total_b, acc_a, acc_b = none, none, empty, empty
        for t in range(tiles):
            total_a = fill(one, t, terms_a, total_a)
            acc_b = weigh(t, terms_b, inverse_b, acc_b)
        put(lax.rem(2 * i + blocks, blocks + 1), acc_b)
        total_a, inverse_a = sums(total_a)
        for t in range(tiles):
            total_b = fill(two, t, terms_b, total_b)
            acc_a = weigh(t, terms_a, inverse_a, acc_a)
        put(2 * i, acc_a)
        total_b, inverse_b = sums(total_b)
        return (
            inverse_b,
            jnp.minimum(least, jnp.min(jnp.minimum(total_a, total_b))),
            jnp.maximum(most, jnp.max(jnp.maximum(total_a, total_b))),
        )

    inverse, least, most = lax.fori_loop(
        0,
        blocks // 2,
        step,
        (jnp.zeros((ROWS, 1), F32), jnp.float32(1.0), jnp.float32(1.0)),
    )
    acc = empty
    for t in range(tiles):
        acc = weigh(t, terms_b, inverse, acc)
    put(blocks - 1, acc)
    safe = jnp.logical_and(least > 2.0**-76, most < 2.0**100)

    @pl.when(jnp.logical_not(safe))
    def _():
        def again(i, _):
            q = qry[i].astype(F32)
            lane = lax.broadcasted_iota(jnp.int32, q.shape, 1)
            q = jnp.where(lane == HEAD, 0.0, q).astype(BF16)
            top = None
            for t in range(tiles):
                s = jnp.dot(q, keys[:, tile(t)], preferred_element_type=F32)
                here = jnp.max(s, axis=-1, keepdims=True)
                top = here if top is None else jnp.maximum(top, here)
            total = none
            for t in range(tiles):
                total = fill(q, t, terms_a, total, top)
            inverse = 1.0 / jnp.sum(total, axis=-1, keepdims=True)
            acc = empty
            for t in range(tiles):
                acc = weigh(t, terms_a, inverse, acc)
            put(i, acc)
            return 0

        lax.fori_loop(0, blocks, again, 0)

    for s, out in enumerate(outs):
        out[...] = found[4 * s : 4 * s + 4]


def regroup_kernel(*refs):
    for m, out in enumerate(refs[4:]):
        for s, part in enumerate(refs[:4]):
            out[s] = part[m]


def project_kernel(at_ref, *refs):
    parts = refs[:4]
    wout_ref, wcq_ref, img_ref, gate_ref, after_ref, cq_ref, wide = refs[4:]
    for d, part in enumerate(parts):
        x = lax.rem(at_ref[1] - d + 4, 4)
        for m in range(4):
            side = lax.bitwise_xor(at_ref[0], m)
            head = (side // 2) * 8 + x * 2 + lax.rem(side, 2)
            wide[pl.ds(pl.multiple_of(head * HEAD, 8), HEAD), :] = part[m].astype(F32)
    projected = jnp.dot(wide[...].T.astype(BF16), wout_ref[...], preferred_element_type=F32)
    after = (img_ref[...].astype(F32) + gate_ref[...] * projected).astype(BF16)
    after_ref[...] = after
    cq_ref[...] = jnp.dot(after, wcq_ref[...], preferred_element_type=F32).astype(BF16)


def cross_kernel(len_ref, cq_ref, after_ref, kv_ref, wco_ref, out_ref, wide):
    length = len_ref[0]
    rows = cq_ref.shape[0]
    visible = lax.broadcasted_iota(jnp.int32, (rows, LT), 1) < length
    for h in range(HEADS):
        qry = cq_ref[:, h * HEAD : (h + 1) * HEAD]
        s = jnp.dot(qry, kv_ref[h], preferred_element_type=F32) * SCORE_SCALE
        s = jnp.where(visible, s, -1e30)
        e = jnp.exp(s - jnp.max(s, axis=-1, keepdims=True))
        p = (e / jnp.sum(e, axis=-1, keepdims=True)).astype(BF16)
        wide[h * HEAD : (h + 1) * HEAD, :] = nt_dot(kv_ref[HEADS + h], p)
    final = jnp.dot(wide[...].T.astype(BF16), wco_ref[...], preferred_element_type=F32)
    out_ref[...] = (after_ref[...].astype(F32) + final).astype(BF16)


def whole(dims):
    return pl.BlockSpec(dims, lambda i: (0,) * len(dims))


def third(k):
    return pl.BlockSpec((W, W), lambda i: (0, k))


def project(at, parts, side, img, gate):
    rows = img.shape[0]
    return pl.pallas_call(
        project_kernel,
        grid=(1,),
        out_shape=[shape((rows, W))] * 2,
        in_specs=[SMEM]
        + [whole(part.shape) for part in parts]
        + [third(0), third(1), whole(img.shape), whole(gate.shape)],
        out_specs=[whole((rows, W))] * 2,
        scratch_shapes=[pltpu.VMEM((W, rows), F32)],
        compiler_params=grant(56),
        cost_estimate=pl.CostEstimate(
            flops=4 * rows * W * W, bytes_accessed=8 << 20, transcendentals=0
        ),
        name="project_out_and_query",
    )(at, *parts, side, side, img, gate)


def cross(length, cq, after, kv, side):
    rows = cq.shape[0]
    return pl.pallas_call(
        cross_kernel,
        grid=(1,),
        out_shape=shape((rows, W)),
        in_specs=[SMEM, whole(cq.shape), whole(after.shape), whole(kv.shape), third(2)],
        out_specs=whole((rows, W)),
        scratch_shapes=[pltpu.VMEM((W, rows), F32)],
        compiler_params=grant(56),
        cost_estimate=pl.CostEstimate(
            flops=4 * rows * W * W, bytes_accessed=5 << 20, transcendentals=rows * LT * HEADS
        ),
        name="cross_attention",
    )(length, cq, after, kv, side)


def local(
    token_ids,
    text_lengths,
    embed_table,
    ff_gain,
    wi_gate,
    wi_up,
    wo_down,
    final_gain,
    cap_weight,
    cap_bias,
    image,
    modulation,
    w_qkv,
    w_out,
    w_cq,
    w_ckv,
    w_co,
):
    plane = lax.axis_size(PLANE)
    place = lax.axis_index(PLANE)
    prompts, tokens = token_ids.shape
    share = tokens // plane
    vocab_rows, feats = embed_table.shape
    units = wi_gate.shape[1]
    width = DT // plane

    local_ids = token_ids.reshape(-1) - place * vocab_rows
    one_hot = (local_ids[:, None] == jnp.arange(vocab_rows, dtype=jnp.int32)[None]).astype(BF16)
    picked = jnp.dot(one_hot, embed_table, preferred_element_type=F32).astype(BF16)
    picked = exchange(picked.reshape(plane, -1, feats), PLANE)

    pixels = image[0]
    rows = pixels.shape[0]
    modulate = modulation[0]
    modulated, head_weight = call(
        modulate_kernel,
        "modulate",
        [shape((rows, W)), shape((3 * HEAD, W))],
        (pixels, modulate, w_qkv.T),
    )
    token_blocks = [modulated] + [shifted(modulated, "x", s) for s in range(1, 4)]
    weight_blocks = [head_weight, crossed(head_weight, "core", 1), crossed(head_weight, "yhi", 1)]
    weight_blocks.append(crossed(weight_blocks[2], "core", 1))
    core, row = lax.axis_index("core"), lax.axis_index("tp")
    at = jnp.stack(
        [lax.axis_index(a) for a in (ROW, "x", "tp", PLANE)] + [lax.bitwise_xor(core, row)]
    ).astype(jnp.int32)
    span = 4 * rows
    made = call(
        qkv_kernel,
        "query_key_value",
        [shape((3 * SLOT, span))] * 4,
        (at, *token_blocks, *weight_blocks),
        scratch=[pltpu.VMEM((span, W), BF16), pltpu.VMEM((4, 3 * HEAD, W), BF16)],
        in_specs=[SMEM] + [VMEM] * 8,
        flops=2 * span * W * 12 * HEAD,
        moved=8 << 20,
        mib=56,
    )
    fulls = [made[0]] + [crossed(made[m], ROW, m) for m in range(1, 4)]
    others = [crossed(full, "core", 1) for full in fulls]

    embedded = call(
        embed_kernel,
        "embed_sum",
        shape(picked.shape),
        (picked,),
        after=(tie(*token_blocks[1:], *weight_blocks[1:]),),
    )
    gate_up, tick = call(
        gate_up_kernel,
        "text_gate_up",
        [shape((prompts, tokens + 2 * share, 2 * units))],
        (at, exchange(embedded, PLANE), ff_gain.reshape(1, feats), wi_gate.T, wi_up.T),
        scratch=[pltpu.VMEM((feats, 2 * units), BF16), pltpu.VMEM((tokens, feats), F32)],
        in_specs=[SMEM] + [VMEM] * 4,
        flops=4 * prompts * tokens * feats * units,
        moved=4 << 20,
        after=(tie(*fulls[1:], *others),),
        tick=True,
    )
    side = call(side_kernel, "side_weights", shape((w_out.shape[0], 3 * W)), (w_out, w_cq, w_co))
    pair = call(
        pair_kernel,
        "side_pair",
        shape((HEAD, 3 * W)),
        (at, side, crossed(side, "tp", 1)),
        in_specs=[SMEM, VMEM, VMEM],
        after=(tick,),
    )
    side = lax.all_gather(pair, SEQ, axis=0, tiled=True)
    *found, attended = call(
        attention_kernel,
        "self_attention",
        [shape((4, HEAD, rows))] * 4,
        (at, *fulls, *others),
        scratch=[
            pltpu.VMEM((2 * SLOT, 8 * span), BF16),
            pltpu.VMEM((8 * span, SLOT), BF16),
            pltpu.VMEM((16, ROWS, 2 * SLOT), BF16),
            pltpu.VMEM((ROWS, 8 * span), F32),
            pltpu.VMEM((ROWS, 8 * span), F32),
            pltpu.VMEM((17, HEAD, ROWS), BF16),
        ],
        in_specs=[SMEM] + [VMEM] * 8,
        flops=16 * span * 2 * span * 256 * 2,
        moved=8 << 20,
        exps=4 * span * 8 * span,
        after=(tick,),
        tick=True,
        mib=56,
    )
    found = [found[0]] + [crossed(found[m], ROW, m) for m in range(1, 4)]
    down = call(
        down_kernel,
        "text_down",
        shape((plane, tokens + 2 * share, width)),
        (exchange(gate_up, "grp"), wo_down),
        flops=2 * tokens * DT * units,
        moved=5 << 20,
        exps=tokens * units,
        after=(attended,),
    )
    cap_part, tick = call(
        cap_kernel,
        "caption_partial",
        [shape((plane, share, W + 128))],
        (exchange(down, PLANE), final_gain.reshape(1, width), cap_weight),
        scratch=[pltpu.VMEM((tokens, width), F32), pltpu.VMEM((tokens, W + 128), F32)],
        tick=True,
    )
    *grouped, tick = call(
        regroup_kernel,
        "regroup",
        [shape((4, HEAD, rows))] * 4,
        tuple(found),
        after=(tick,),
        tick=True,
    )
    caption = call(
        caption_kernel,
        "caption",
        shape((plane, share, W)),
        (exchange(cap_part, PLANE), cap_bias.reshape(1, W)),
        after=(tick,),
    )
    parts = [grouped[0]] + [shifted(grouped[d], "x", d) for d in range(1, 4)]
    after_self, cross_query = project(at, parts, side, pixels, modulate[2:3])
    kv_part = call(
        kv_kernel,
        "text_kv",
        shape((plane, w_ckv.shape[1], tokens)),
        (exchange(caption, PLANE), w_ckv.T),
        scratch=[pltpu.VMEM((tokens, W), F32)],
        after=(tie(*(part[0] for part in parts[1:])),),
    )
    text_kv = exchange(kv_part, PLANE)
    result = cross(text_lengths, cross_query, after_self, text_kv, side)
    return result[None]


def solution(mesh):
    grp, seq, tp = mesh.devices.shape
    fine = Mesh(mesh.devices.reshape(grp, 2, seq // 4, 2, tp), ("grp",) + PLANE)
    placed = (
        P(),
        P("grp"),
        P(PLANE, "grp"),
        P("grp"),
        P("grp", PLANE),
        P("grp", PLANE),
        P(PLANE, None),
        P(PLANE),
        P(PLANE, None),
        P(),
        P("grp", PLANE, None),
        P("grp", None, None),
        P(None, SEQ),
        P(PLANE, None),
        P(PLANE, None),
        P(None, PLANE),
        P(PLANE, None),
    )
    return jax.shard_map(
        local, mesh=fine, in_specs=placed, out_specs=P("grp", PLANE, None), check_vma=False
    )
```

```python
import math

import jax
import jax.numpy as jnp
from jax import lax
from jax.experimental import pallas as pl
from jax.experimental.pallas import tpu as pltpu
from jax.sharding import Mesh
from jax.sharding import PartitionSpec as P

W = 1152
HEADS = 16
DT = 4096
HEAD = 72
SLOT = 80
LT = 128
EPSILON = 1e-06
PLANE = ("yhi", "x", "core", "tp")
SEQ = ("yhi", "x", "core")
SIDE = ("yhi", "core")
ROW = ("yhi", "tp")
SCORE_SCALE = 1.0 / math.sqrt(HEAD)
EXP2_SCALE = SCORE_SCALE * math.log2(math.e)
LIFT = 64.0
F32 = jnp.float32
BF16 = jnp.bfloat16

VMEM = pl.BlockSpec(memory_space=pltpu.VMEM)
SMEM = pl.BlockSpec(memory_space=pltpu.SMEM)


def grant(mib):
    return pltpu.CompilerParams(vmem_limit_bytes=mib * 1024 * 1024)


def gelu_tanh(values):
    return jax.nn.gelu(values, approximate=True)


def exchange(blocks, axes):
    return lax.all_to_all(blocks, axes, 0, 0, tiled=True)


def shifted(value, axis, shift):
    size = lax.axis_size(axis)
    return lax.ppermute(value, axis, [(i, (i + shift) % size) for i in range(size)])


def crossed(value, axis, mask):
    size = lax.axis_size(axis)
    return lax.ppermute(value, axis, [(i, i ^ mask) for i in range(size)])


def nt_dot(a, b):
    return lax.dot_general(a, b, (((1,), (1,)), ((), ())), preferred_element_type=F32)


def thirds(values):
    high = values.astype(BF16).astype(F32)
    mid = (values - high).astype(BF16).astype(F32)
    return high, mid, values - high - mid


TICK = (8, 128)


def call(
    kernel,
    name,
    out_shape,
    args,
    scratch=(),
    in_specs=None,
    flops=0,
    moved=1 << 20,
    exps=0,
    after=(),
    tick=False,
    mib=16,
):
    outs = list(out_shape) if isinstance(out_shape, list) else [out_shape]
    many = tick or isinstance(out_shape, list)
    if tick:
        outs.append(shape(TICK, F32))
    first, waits = len(args), len(after)
    last = first + waits + len(outs)

    def body(*refs):
        if tick:
            refs[last - 1][...] = jnp.zeros(TICK, F32)
        kernel(*refs[:first], *refs[first + waits : last - tick], *refs[last:])

    return pl.pallas_call(
        body,
        out_shape=outs if many else outs[0],
        in_specs=(in_specs or [VMEM] * len(args)) + [VMEM] * waits,
        out_specs=[VMEM] * len(outs) if many else VMEM,
        scratch_shapes=list(scratch),
        compiler_params=grant(mib),
        cost_estimate=pl.CostEstimate(flops=flops, bytes_accessed=moved, transcendentals=exps),
        name=name,
    )(*args, *after)


def tie(*arrays):
    total = jnp.zeros(TICK, F32)
    for array in arrays:
        total = total + array[: TICK[0], : TICK[1]].astype(F32)
    return total


def shape(dims, dtype=BF16):
    return jax.ShapeDtypeStruct(dims, dtype)


def embed_kernel(in_ref, out_ref):
    total = in_ref[0].astype(F32)
    for j in range(1, in_ref.shape[0]):
        total += in_ref[j].astype(F32)
    total = total.astype(BF16)
    for j in range(out_ref.shape[0]):
        out_ref[j] = total


def row_of(column):
    return jnp.broadcast_to(column, (column.shape[0], 128)).T[:1]


def column_of(row):
    return jnp.broadcast_to(row, (128, row.shape[1])).T[:, :1]


def gate_up_kernel(
    at_ref, in_ref, gain_ref, gate_ref, up_ref, side_ref, other_ref, out_ref, pair_ref, weight, rows32
):
    own, other = side_ref[...].astype(F32), other_ref[...].astype(F32)
    first = at_ref[2] == 0
    pair_ref[...] = jnp.concatenate(
        [jnp.where(first, own, other), jnp.where(first, other, own)], axis=0
    ).astype(BF16)
    prompts, _, both = out_ref.shape
    plane, group, feats = in_ref.shape
    tokens = plane * group // prompts
    share = tokens // plane
    weight[...] = (
        jnp.concatenate([gate_ref[...].astype(F32), up_ref[...].astype(F32)], axis=0)
        .T.astype(BF16)
    )
    per = plane // prompts
    at = at_ref[3] * share
    base = pl.multiple_of(at // 8 * 8, 8)
    upper = lax.rem(at, 8) == 0
    for p in range(prompts):
        rows = in_ref[p * per : (p + 1) * per].reshape(tokens, feats).astype(F32)
        rows32[...] = rows
        scaled = (rows * gain_ref[...]).astype(BF16)
        out_ref[p, :tokens, :] = jnp.dot(
            scaled, weight[...], preferred_element_type=F32
        ).astype(BF16)
        near = rows32[pl.ds(base, 8), :]
        own = jnp.where(upper, near[:share], near[share:])
        square = row_of(jnp.sum(rows * rows, axis=-1, keepdims=True))
        squares = jnp.concatenate(list(thirds(square)) + [jnp.zeros_like(square)], axis=0)
        out_ref[p, tokens:, :] = jnp.concatenate(
            [
                jnp.concatenate([own, jnp.zeros((share, both - feats), F32)], axis=1),
                jnp.concatenate([squares, jnp.zeros((4, both - tokens), F32)], axis=1),
            ],
            axis=0,
        ).astype(BF16)


def down_kernel(in_ref, down_ref, out_ref):
    groups, rows, both = in_ref.shape
    plane, _, width = out_ref.shape
    tokens = 128
    share = tokens // plane
    units = down_ref.shape[0]
    feats = DT // groups
    total = in_ref[0, :tokens, :].astype(F32)
    square = None
    for g in range(groups):
        if g:
            total += in_ref[g, :tokens, :].astype(F32)
        extra = in_ref[g, tokens:, :].astype(F32)
        for i in range(3):
            part = extra[share + i : share + i + 1, :tokens]
            square = part if square is None else square + part
        for k in range(feats // width):
            piece = extra[:share, k * width : (k + 1) * width]
            out_ref[g * (feats // width) + k, tokens:, :] = jnp.concatenate(
                [piece, jnp.zeros_like(piece)], axis=0
            ).astype(BF16)
    inverse = column_of(lax.rsqrt(square / DT + EPSILON))
    total = total * inverse
    hidden = (gelu_tanh(total[:, :units]) * total[:, units:]).astype(BF16)
    step = 4
    for j in range(0, plane, step):
        part = jnp.dot(
            hidden, down_ref[:, j * width : (j + step) * width], preferred_element_type=F32
        ).astype(BF16)
        for k in range(step):
            out_ref[j + k, :tokens, :] = part[:, k * width : (k + 1) * width]


def cap_kernel(in_ref, gain_ref, weight_ref, out_ref, rest, wide):
    plane, share, _ = out_ref.shape
    tokens = plane * share
    total = in_ref[0, :tokens, :].astype(F32)
    for j in range(1, plane):
        total += in_ref[j, :tokens, :].astype(F32)
    for j in range(plane):
        rest[j * share : (j + 1) * share, :] = in_ref[j, tokens:, :].astype(F32)[:share]
    state = total + rest[...]
    high, mid, low = thirds(jnp.sum(state * state, axis=-1, keepdims=True))
    lane = lax.broadcasted_iota(jnp.int32, (tokens, wide.shape[1] - W), 1)
    wide[:, W:] = jnp.where(
        lane == 0, high, jnp.where(lane == 1, mid, jnp.where(lane == 2, low, 0.0))
    )
    gained = (state * gain_ref[...]).astype(BF16)
    wide[:, :W] = jnp.dot(gained, weight_ref[...], preferred_element_type=F32)
    for j in range(plane):
        out_ref[j] = wide[j * share : (j + 1) * share, :].astype(BF16)


def caption_kernel(in_ref, bias_ref, out_ref):
    total = in_ref[0].astype(F32)
    for j in range(1, in_ref.shape[0]):
        total += in_ref[j].astype(F32)
    square = total[:, W : W + 1] + total[:, W + 1 : W + 2] + total[:, W + 2 : W + 3]
    inverse = lax.rsqrt(square / DT + EPSILON)
    caption = gelu_tanh(total[:, :W] * inverse + bias_ref[...]).astype(BF16)
    for j in range(out_ref.shape[0]):
        out_ref[j] = caption


def kv_kernel(in_ref, weight_ref, out_ref, rows):
    plane, share, _ = in_ref.shape
    for j in range(plane):
        rows[j * share : (j + 1) * share, :] = in_ref[j].astype(F32)
    kv = nt_dot(weight_ref[...], rows[...].astype(BF16)).astype(BF16)
    for j in range(plane):
        out_ref[j] = kv


def modulate_kernel(image_ref, mod_ref, weight_ref, out_ref, copy_ref):
    copy_ref[...] = weight_ref[...]
    pixels = image_ref[...].astype(F32)
    center = jnp.mean(pixels, axis=-1, keepdims=True)
    spread = jnp.mean((pixels - center) ** 2, axis=-1, keepdims=True)
    out_ref[...] = (
        (pixels - center) * lax.rsqrt(spread + EPSILON) * (1.0 + mod_ref[1:2]) + mod_ref[0:1]
    ).astype(BF16)


def side_kernel(*refs):
    out_ref = refs[-1]
    for k, ref in enumerate(refs[:-1]):
        out_ref[:, k * W : (k + 1) * W] = ref[...]


def qkv_kernel(at_ref, *refs):
    tokens, weights = refs[:4], refs[4:8]
    fulls = refs[8:12]
    x_rows, by_chip = refs[12:14]
    rows = tokens[0].shape[0]
    for m, block in enumerate(tokens):
        at = lax.rem(at_ref[1] - m + 4, 4)
        x_rows[pl.ds(pl.multiple_of(at * rows, rows), rows), :] = block[...]
    for m, block in enumerate(weights):
        by_chip[lax.bitwise_xor(at_ref[4], m)] = block[...]
    span = x_rows.shape[0]
    zeros = jnp.zeros((SLOT - HEAD, span), F32)
    ones = (lax.broadcasted_iota(jnp.int32, zeros.shape, 0) == 0).astype(F32)
    for s in range(4):
        out = nt_dot(by_chip[s], x_rows[...])
        for i, tail in enumerate((zeros, ones, zeros)):
            fulls[s][i * SLOT : (i + 1) * SLOT, :] = jnp.concatenate(
                [out[i * HEAD : (i + 1) * HEAD], tail], axis=0
            ).astype(BF16)


ROWS = 192
TILE = 256


def attention_kernel(at_ref, *refs):
    fulls, others = refs[:4], refs[4:8]
    outs = refs[8:12]
    keys, vals, qry, terms_a, terms_b, found = refs[12:18]
    span = fulls[0].shape[1]
    count = 8 * span
    largest = None
    for c, ref in enumerate(fulls + others):
        block = ref[SLOT : 2 * SLOT, :]
        cols = slice(c * span, (c + 1) * span)
        keys[:SLOT, cols] = block
        keys[SLOT:, cols] = block
        vals[cols, :] = ref[2 * SLOT : 3 * SLOT, :].astype(F32).T.astype(BF16)
        wide = block.astype(F32)
        row = lax.broadcasted_iota(jnp.int32, wide.shape, 0)
        norm = jnp.sum(jnp.where(row < HEAD, wide * wide, 0.0), axis=0, keepdims=True)
        largest = norm if largest is None else jnp.maximum(largest, norm)
    largest = jnp.max(largest, axis=-1, keepdims=True)
    for s in range(4):
        q = fulls[s][0:SLOT, :].astype(F32) * SCORE_SCALE
        high = q.astype(BF16).astype(F32)
        row = lax.broadcasted_iota(jnp.int32, q.shape, 0)
        bound = jnp.sqrt(jnp.sum(q * q, axis=0, keepdims=True) * largest) * (1.0 + 2.0**-6)
        high = jnp.where(row == HEAD, LIFT * math.log(2.0) - bound, high)
        low = jnp.where(row == HEAD, 0.0, q - high)
        both = jnp.concatenate([high, low], axis=0).T
        for a in range(4):
            away = lax.rem(a - at_ref[1] + 4, 4)
            qry[s * 4 + away] = both[a * ROWS : (a + 1) * ROWS].astype(BF16)

    def tile(t):
        return slice(t * TILE, (t + 1) * TILE)

    def fill(q, t, terms, total, shift=None):
        s = jnp.dot(q, keys[:, tile(t)], preferred_element_type=F32)
        e = jnp.exp(s if shift is None else s - shift)
        terms[:, tile(t)] = e
        return total + (e[:, :128] + e[:, 128:])

    def weigh(t, terms, inverse, acc):
        p = (terms[:, tile(t)] * inverse).astype(BF16)
        return acc + jnp.dot(p, vals[tile(t), :], preferred_element_type=F32)

    def put(i, acc):
        found[i] = acc.T[:HEAD].astype(BF16)

    tiles = count // TILE
    none = jnp.zeros((ROWS, 128), F32)
    empty = jnp.zeros((ROWS, SLOT), F32)

    def sums(total):
        total = jnp.sum(total, axis=-1, keepdims=True)
        return total, 1.0 / total

    blocks = qry.shape[0]
    terms_b[...] = jnp.zeros(terms_b.shape, F32)

    def step(i, carry):
        inverse_b, least, most = carry
        one, two = qry[2 * i], qry[2 * i + 1]
        total_a, total_b, acc_a, acc_b = none, none, empty, empty
        for t in range(tiles):
            total_a = fill(one, t, terms_a, total_a)
            acc_b = weigh(t, terms_b, inverse_b, acc_b)
        put(lax.rem(2 * i + blocks, blocks + 1), acc_b)
        total_a, inverse_a = sums(total_a)
        for t in range(tiles):
            total_b = fill(two, t, terms_b, total_b)
            acc_a = weigh(t, terms_a, inverse_a, acc_a)
        put(2 * i, acc_a)
        total_b, inverse_b = sums(total_b)
        return (
            inverse_b,
            jnp.minimum(least, jnp.min(jnp.minimum(total_a, total_b))),
            jnp.maximum(most, jnp.max(jnp.maximum(total_a, total_b))),
        )

    inverse, least, most = lax.fori_loop(
        0,
        blocks // 2,
        step,
        (jnp.zeros((ROWS, 1), F32), jnp.float32(1.0), jnp.float32(1.0)),
    )
    acc = empty
    for t in range(tiles):
        acc = weigh(t, terms_b, inverse, acc)
    put(blocks - 1, acc)
    safe = jnp.logical_and(least > 2.0**-76, most < 2.0**100)

    @pl.when(jnp.logical_not(safe))
    def _():
        def again(i, _):
            q = qry[i].astype(F32)
            lane = lax.broadcasted_iota(jnp.int32, q.shape, 1)
            q = jnp.where(lane == HEAD, 0.0, q).astype(BF16)
            top = None
            for t in range(tiles):
                s = jnp.dot(q, keys[:, tile(t)], preferred_element_type=F32)
                here = jnp.max(s, axis=-1, keepdims=True)
                top = here if top is None else jnp.maximum(top, here)
            total = none
            for t in range(tiles):
                total = fill(q, t, terms_a, total, top)
            inverse = 1.0 / jnp.sum(total, axis=-1, keepdims=True)
            acc = empty
            for t in range(tiles):
                acc = weigh(t, terms_a, inverse, acc)
            put(i, acc)
            return 0

        lax.fori_loop(0, blocks, again, 0)

    for s, out in enumerate(outs):
        out[...] = found[4 * s : 4 * s + 4]


def regroup_kernel(*refs):
    for m, out in enumerate(refs[4:]):
        for s, part in enumerate(refs[:4]):
            out[s] = part[m]


def project_kernel(at_ref, *refs):
    parts = refs[:4]
    wout_ref, wcq_ref, img_ref, gate_ref, after_ref, cq_ref, wide = refs[4:]
    for d, part in enumerate(parts):
        x = lax.rem(at_ref[1] - d + 4, 4)
        for m in range(4):
            side = lax.bitwise_xor(at_ref[0], m)
            head = (side // 2) * 8 + x * 2 + lax.rem(side, 2)
            wide[pl.ds(pl.multiple_of(head * HEAD, 8), HEAD), :] = part[m].astype(F32)
    projected = jnp.dot(wide[...].T.astype(BF16), wout_ref[...], preferred_element_type=F32)
    after = (img_ref[...].astype(F32) + gate_ref[...] * projected).astype(BF16)
    after_ref[...] = after
    cq_ref[...] = jnp.dot(after, wcq_ref[...], preferred_element_type=F32).astype(BF16)


def cross_kernel(len_ref, cq_ref, after_ref, kv_ref, wco_ref, out_ref, wide):
    length = len_ref[0]
    rows = cq_ref.shape[0]
    visible = lax.broadcasted_iota(jnp.int32, (rows, LT), 1) < length
    for h in range(HEADS):
        qry = cq_ref[:, h * HEAD : (h + 1) * HEAD]
        s = jnp.dot(qry, kv_ref[h], preferred_element_type=F32) * SCORE_SCALE
        s = jnp.where(visible, s, -1e30)
        e = jnp.exp(s - jnp.max(s, axis=-1, keepdims=True))
        p = (e / jnp.sum(e, axis=-1, keepdims=True)).astype(BF16)
        wide[h * HEAD : (h + 1) * HEAD, :] = nt_dot(kv_ref[HEADS + h], p)
    final = jnp.dot(wide[...].T.astype(BF16), wco_ref[...], preferred_element_type=F32)
    out_ref[...] = (after_ref[...].astype(F32) + final).astype(BF16)


def whole(dims):
    return pl.BlockSpec(dims, lambda i: (0,) * len(dims))


def third(k):
    return pl.BlockSpec((W, W), lambda i: (0, k))


def project(at, parts, side, img, gate):
    rows = img.shape[0]
    return pl.pallas_call(
        project_kernel,
        grid=(1,),
        out_shape=[shape((rows, W))] * 2,
        in_specs=[SMEM]
        + [whole(part.shape) for part in parts]
        + [third(0), third(1), whole(img.shape), whole(gate.shape)],
        out_specs=[whole((rows, W))] * 2,
        scratch_shapes=[pltpu.VMEM((W, rows), F32)],
        compiler_params=grant(24),
        cost_estimate=pl.CostEstimate(
            flops=4 * rows * W * W, bytes_accessed=8 << 20, transcendentals=0
        ),
        name="project_out_and_query",
    )(at, *parts, side, side, img, gate)


def cross(length, cq, after, kv, side):
    rows = cq.shape[0]
    return pl.pallas_call(
        cross_kernel,
        grid=(1,),
        out_shape=shape((rows, W)),
        in_specs=[SMEM, whole(cq.shape), whole(after.shape), whole(kv.shape), third(2)],
        out_specs=whole((rows, W)),
        scratch_shapes=[pltpu.VMEM((W, rows), F32)],
        compiler_params=grant(16),
        cost_estimate=pl.CostEstimate(
            flops=4 * rows * W * W, bytes_accessed=5 << 20, transcendentals=rows * LT * HEADS
        ),
        name="cross_attention",
    )(length, cq, after, kv, side)


def local(
    token_ids,
    text_lengths,
    embed_table,
    ff_gain,
    wi_gate,
    wi_up,
    wo_down,
    final_gain,
    cap_weight,
    cap_bias,
    image,
    modulation,
    w_qkv,
    w_out,
    w_cq,
    w_ckv,
    w_co,
):
    plane = lax.axis_size(PLANE)
    place = lax.axis_index(PLANE)
    prompts, tokens = token_ids.shape
    share = tokens // plane
    vocab_rows, feats = embed_table.shape
    units = wi_gate.shape[1]
    width = DT // plane

    local_ids = token_ids.reshape(-1) - place * vocab_rows
    one_hot = (local_ids[:, None] == jnp.arange(vocab_rows, dtype=jnp.int32)[None]).astype(BF16)
    picked = jnp.dot(one_hot, embed_table, preferred_element_type=F32).astype(BF16)
    picked = exchange(picked.reshape(plane, -1, feats), PLANE)

    pixels = image[0]
    rows = pixels.shape[0]
    modulate = modulation[0]
    modulated, head_weight = call(
        modulate_kernel,
        "modulate",
        [shape((rows, W)), shape((3 * HEAD, W))],
        (pixels, modulate, w_qkv.T),
    )
    token_blocks = [modulated] + [shifted(modulated, "x", s) for s in range(1, 4)]
    weight_blocks = [head_weight, crossed(head_weight, "core", 1), crossed(head_weight, "yhi", 1)]
    weight_blocks.append(crossed(weight_blocks[2], "core", 1))
    core, row = lax.axis_index("core"), lax.axis_index("tp")
    at = jnp.stack(
        [lax.axis_index(a) for a in (ROW, "x", "tp", PLANE)] + [lax.bitwise_xor(core, row)]
    ).astype(jnp.int32)
    span = 4 * rows
    made = call(
        qkv_kernel,
        "query_key_value",
        [shape((3 * SLOT, span))] * 4,
        (at, *token_blocks, *weight_blocks),
        scratch=[pltpu.VMEM((span, W), BF16), pltpu.VMEM((4, 3 * HEAD, W), BF16)],
        in_specs=[SMEM] + [VMEM] * 8,
        flops=2 * span * W * 12 * HEAD,
        moved=8 << 20,
        mib=56,
    )
    fulls = [made[0]] + [crossed(made[m], ROW, m) for m in range(1, 4)]
    others = [crossed(full, "core", 1) for full in fulls]

    embedded = call(
        embed_kernel,
        "embed_sum",
        shape(picked.shape),
        (picked,),
        after=(tie(*token_blocks[1:], *weight_blocks[1:3]),),
    )
    side = call(side_kernel, "side_weights", shape((w_out.shape[0], 3 * W)), (w_out, w_cq, w_co))
    gate_up, pair, tick = call(
        gate_up_kernel,
        "text_gate_up",
        [shape((prompts, tokens + 2 * share, 2 * units)), shape((HEAD, 3 * W))],
        (
            at,
            exchange(embedded, PLANE),
            ff_gain.reshape(1, feats),
            wi_gate.T,
            wi_up.T,
            side,
            crossed(side, "tp", 1),
        ),
        scratch=[pltpu.VMEM((feats, 2 * units), BF16), pltpu.VMEM((tokens, feats), F32)],
        in_specs=[SMEM] + [VMEM] * 6,
        flops=4 * prompts * tokens * feats * units,
        moved=4 << 20,
        after=(tie(*fulls[1:], *others),),
        tick=True,
        mib=20,
    )
    side = lax.all_gather(pair, SEQ, axis=0, tiled=True)
    *found, attended = call(
        attention_kernel,
        "self_attention",
        [shape((4, HEAD, rows))] * 4,
        (at, *fulls, *others),
        scratch=[
            pltpu.VMEM((2 * SLOT, 8 * span), BF16),
            pltpu.VMEM((8 * span, SLOT), BF16),
            pltpu.VMEM((16, ROWS, 2 * SLOT), BF16),
            pltpu.VMEM((ROWS, 8 * span), F32),
            pltpu.VMEM((ROWS, 8 * span), F32),
            pltpu.VMEM((17, HEAD, ROWS), BF16),
        ],
        in_specs=[SMEM] + [VMEM] * 8,
        flops=16 * span * 2 * span * 256 * 2,
        moved=8 << 20,
        exps=4 * span * 8 * span,
        after=(tick,),
        tick=True,
        mib=56,
    )
    found = [found[0]] + [crossed(found[m], ROW, m) for m in range(1, 4)]
    down = call(
        down_kernel,
        "text_down",
        shape((plane, tokens + 2 * share, width)),
        (exchange(gate_up, "grp"), wo_down),
        flops=2 * tokens * DT * units,
        moved=5 << 20,
        exps=tokens * units,
        after=(attended,),
    )
    cap_part = call(
        cap_kernel,
        "caption_partial",
        shape((plane, share, W + 128)),
        (exchange(down, PLANE), final_gain.reshape(1, width), cap_weight),
        scratch=[pltpu.VMEM((tokens, width), F32), pltpu.VMEM((tokens, W + 128), F32)],
    )
    grouped = call(
        regroup_kernel,
        "regroup",
        [shape((4, HEAD, rows))] * 4,
        tuple(found),
    )
    caption = call(
        caption_kernel,
        "caption",
        shape((plane, share, W)),
        (exchange(cap_part, PLANE), cap_bias.reshape(1, W)),
    )
    parts = [grouped[0]] + [shifted(grouped[d], "x", d) for d in range(1, 4)]
    after_self, cross_query = project(at, parts, side, pixels, modulate[2:3])
    kv_part = call(
        kv_kernel,
        "text_kv",
        shape((plane, w_ckv.shape[1], tokens)),
        (exchange(caption, PLANE), w_ckv.T),
        scratch=[pltpu.VMEM((tokens, W), F32)],
        after=(tie(*(part[0] for part in parts[1:])),),
    )
    text_kv = exchange(kv_part, PLANE)
    result = cross(text_lengths, cross_query, after_self, text_kv, side)
    return result[None]


def solution(mesh):
    grp, seq, tp = mesh.devices.shape
    fine = Mesh(mesh.devices.reshape(grp, 2, seq // 4, 2, tp), ("grp",) + PLANE)
    placed = (
        P(),
        P("grp"),
        P(PLANE, "grp"),
        P("grp"),
        P("grp", PLANE),
        P("grp", PLANE),
        P(PLANE, None),
        P(PLANE),
        P(PLANE, None),
        P(),
        P("grp", PLANE, None),
        P("grp", None, None),
        P(None, SEQ),
        P(PLANE, None),
        P(PLANE, None),
        P(None, PLANE),
        P(PLANE, None),
    )
    return jax.shard_map(
        local, mesh=fine, in_specs=placed, out_specs=P("grp", PLANE, None), check_vma=False
    )
```

```python
import math

import jax
import jax.numpy as jnp
from jax import lax
from jax.experimental import pallas as pl
from jax.experimental.pallas import tpu as pltpu
from jax.sharding import Mesh
from jax.sharding import PartitionSpec as P

W = 1152
HEADS = 16
DT = 4096
HEAD = 72
SLOT = 80
LT = 128
EPSILON = 1e-06
PLANE = ("yhi", "x", "core", "tp")
SEQ = ("yhi", "x", "core")
SIDE = ("yhi", "core")
ROW = ("yhi", "tp")
SCORE_SCALE = 1.0 / math.sqrt(HEAD)
EXP2_SCALE = SCORE_SCALE * math.log2(math.e)
LIFT = 64.0
F32 = jnp.float32
BF16 = jnp.bfloat16

VMEM = pl.BlockSpec(memory_space=pltpu.VMEM)
SMEM = pl.BlockSpec(memory_space=pltpu.SMEM)


def grant(mib):
    return pltpu.CompilerParams(vmem_limit_bytes=mib * 1024 * 1024)


def gelu_tanh(values):
    return jax.nn.gelu(values, approximate=True)


def exchange(blocks, axes):
    return lax.all_to_all(blocks, axes, 0, 0, tiled=True)


def shifted(value, axis, shift):
    size = lax.axis_size(axis)
    return lax.ppermute(value, axis, [(i, (i + shift) % size) for i in range(size)])


def crossed(value, axis, mask):
    size = lax.axis_size(axis)
    return lax.ppermute(value, axis, [(i, i ^ mask) for i in range(size)])


def nt_dot(a, b):
    return lax.dot_general(a, b, (((1,), (1,)), ((), ())), preferred_element_type=F32)


def thirds(values):
    high = values.astype(BF16).astype(F32)
    mid = (values - high).astype(BF16).astype(F32)
    return high, mid, values - high - mid


TICK = (8, 128)


def call(
    kernel,
    name,
    out_shape,
    args,
    scratch=(),
    in_specs=None,
    flops=0,
    moved=1 << 20,
    exps=0,
    after=(),
    tick=False,
    mib=16,
):
    outs = list(out_shape) if isinstance(out_shape, list) else [out_shape]
    many = tick or isinstance(out_shape, list)
    if tick:
        outs.append(shape(TICK, F32))
    first, waits = len(args), len(after)
    last = first + waits + len(outs)

    def body(*refs):
        if tick:
            refs[last - 1][...] = jnp.zeros(TICK, F32)
        kernel(*refs[:first], *refs[first + waits : last - tick], *refs[last:])

    return pl.pallas_call(
        body,
        out_shape=outs if many else outs[0],
        in_specs=(in_specs or [VMEM] * len(args)) + [VMEM] * waits,
        out_specs=[VMEM] * len(outs) if many else VMEM,
        scratch_shapes=list(scratch),
        compiler_params=grant(mib),
        cost_estimate=pl.CostEstimate(flops=flops, bytes_accessed=moved, transcendentals=exps),
        name=name,
    )(*args, *after)


def tie(*arrays):
    total = jnp.zeros(TICK, F32)
    for array in arrays:
        total = total + array[: TICK[0], : TICK[1]].astype(F32)
    return total


def shape(dims, dtype=BF16):
    return jax.ShapeDtypeStruct(dims, dtype)


def embed_kernel(in_ref, out_ref):
    total = in_ref[0].astype(F32)
    for j in range(1, in_ref.shape[0]):
        total += in_ref[j].astype(F32)
    total = total.astype(BF16)
    for j in range(out_ref.shape[0]):
        out_ref[j] = total


def row_of(column):
    return jnp.broadcast_to(column, (column.shape[0], 128)).T[:1]


def column_of(row):
    return jnp.broadcast_to(row, (128, row.shape[1])).T[:, :1]


def gate_up_kernel(
    at_ref, in_ref, gain_ref, gate_ref, up_ref, side_ref, other_ref, out_ref, pair_ref, weight, rows32
):
    own, other = side_ref[...].astype(F32), other_ref[...].astype(F32)
    first = at_ref[2] == 0
    pair_ref[...] = jnp.concatenate(
        [jnp.where(first, own, other), jnp.where(first, other, own)], axis=0
    ).astype(BF16)
    prompts, _, both = out_ref.shape
    plane, group, feats = in_ref.shape
    tokens = plane * group // prompts
    share = tokens // plane
    weight[...] = (
        jnp.concatenate([gate_ref[...].astype(F32), up_ref[...].astype(F32)], axis=0)
        .T.astype(BF16)
    )
    per = plane // prompts
    at = at_ref[3] * share
    base = pl.multiple_of(at // 8 * 8, 8)
    upper = lax.rem(at, 8) == 0
    for p in range(prompts):
        rows = in_ref[p * per : (p + 1) * per].reshape(tokens, feats).astype(F32)
        rows32[...] = rows
        scaled = (rows * gain_ref[...]).astype(BF16)
        out_ref[p, :tokens, :] = jnp.dot(
            scaled, weight[...], preferred_element_type=F32
        ).astype(BF16)
        near = rows32[pl.ds(base, 8), :]
        own = jnp.where(upper, near[:share], near[share:])
        square = row_of(jnp.sum(rows * rows, axis=-1, keepdims=True))
        squares = jnp.concatenate(list(thirds(square)) + [jnp.zeros_like(square)], axis=0)
        out_ref[p, tokens:, :] = jnp.concatenate(
            [
                jnp.concatenate([own, jnp.zeros((share, both - feats), F32)], axis=1),
                jnp.concatenate([squares, jnp.zeros((4, both - tokens), F32)], axis=1),
            ],
            axis=0,
        ).astype(BF16)


def down_kernel(in_ref, down_ref, out_ref):
    groups, rows, both = in_ref.shape
    plane, _, width = out_ref.shape
    tokens = 128
    share = tokens // plane
    units = down_ref.shape[0]
    feats = DT // groups
    total = in_ref[0, :tokens, :].astype(F32)
    square = None
    for g in range(groups):
        if g:
            total += in_ref[g, :tokens, :].astype(F32)
        extra = in_ref[g, tokens:, :].astype(F32)
        for i in range(3):
            part = extra[share + i : share + i + 1, :tokens]
            square = part if square is None else square + part
        for k in range(feats // width):
            piece = extra[:share, k * width : (k + 1) * width]
            out_ref[g * (feats // width) + k, tokens:, :] = jnp.concatenate(
                [piece, jnp.zeros_like(piece)], axis=0
            ).astype(BF16)
    inverse = column_of(lax.rsqrt(square / DT + EPSILON))
    total = total * inverse
    hidden = (gelu_tanh(total[:, :units]) * total[:, units:]).astype(BF16)
    step = 4
    for j in range(0, plane, step):
        part = jnp.dot(
            hidden, down_ref[:, j * width : (j + step) * width], preferred_element_type=F32
        ).astype(BF16)
        for k in range(step):
            out_ref[j + k, :tokens, :] = part[:, k * width : (k + 1) * width]


def cap_kernel(in_ref, gain_ref, weight_ref, out_ref, rest, wide):
    plane, share, _ = out_ref.shape
    tokens = plane * share
    total = in_ref[0, :tokens, :].astype(F32)
    for j in range(1, plane):
        total += in_ref[j, :tokens, :].astype(F32)
    for j in range(plane):
        rest[j * share : (j + 1) * share, :] = in_ref[j, tokens:, :].astype(F32)[:share]
    state = total + rest[...]
    high, mid, low = thirds(jnp.sum(state * state, axis=-1, keepdims=True))
    lane = lax.broadcasted_iota(jnp.int32, (tokens, wide.shape[1] - W), 1)
    wide[:, W:] = jnp.where(
        lane == 0, high, jnp.where(lane == 1, mid, jnp.where(lane == 2, low, 0.0))
    )
    gained = (state * gain_ref[...]).astype(BF16)
    wide[:, :W] = jnp.dot(gained, weight_ref[...], preferred_element_type=F32)
    for j in range(plane):
        out_ref[j] = wide[j * share : (j + 1) * share, :].astype(BF16)


def caption_kernel(in_ref, bias_ref, out_ref):
    total = in_ref[0].astype(F32)
    for j in range(1, in_ref.shape[0]):
        total += in_ref[j].astype(F32)
    square = total[:, W : W + 1] + total[:, W + 1 : W + 2] + total[:, W + 2 : W + 3]
    inverse = lax.rsqrt(square / DT + EPSILON)
    caption = gelu_tanh(total[:, :W] * inverse + bias_ref[...]).astype(BF16)
    for j in range(out_ref.shape[0]):
        out_ref[j] = caption


def kv_kernel(in_ref, weight_ref, out_ref, rows):
    plane, share, _ = in_ref.shape
    for j in range(plane):
        rows[j * share : (j + 1) * share, :] = in_ref[j].astype(F32)
    kv = nt_dot(weight_ref[...], rows[...].astype(BF16)).astype(BF16)
    for j in range(plane):
        out_ref[j] = kv


def modulate_kernel(image_ref, mod_ref, weight_ref, out_ref, copy_ref):
    copy_ref[...] = weight_ref[...]
    pixels = image_ref[...].astype(F32)
    center = jnp.mean(pixels, axis=-1, keepdims=True)
    spread = jnp.mean((pixels - center) ** 2, axis=-1, keepdims=True)
    out_ref[...] = (
        (pixels - center) * lax.rsqrt(spread + EPSILON) * (1.0 + mod_ref[1:2]) + mod_ref[0:1]
    ).astype(BF16)


def side_kernel(*refs):
    out_ref = refs[-1]
    for k, ref in enumerate(refs[:-1]):
        out_ref[:, k * W : (k + 1) * W] = ref[...]


def qkv_kernel(at_ref, *refs):
    tokens, weights = refs[:4], refs[4:8]
    fulls = refs[8:12]
    x_rows, by_chip = refs[12:14]
    rows = tokens[0].shape[0]
    for m, block in enumerate(tokens):
        at = lax.rem(at_ref[1] - m + 4, 4)
        x_rows[pl.ds(pl.multiple_of(at * rows, rows), rows), :] = block[...]
    for m, block in enumerate(weights):
        by_chip[lax.bitwise_xor(at_ref[4], m)] = block[...]
    span = x_rows.shape[0]
    zeros = jnp.zeros((SLOT - HEAD, span), F32)
    ones = (lax.broadcasted_iota(jnp.int32, zeros.shape, 0) == 0).astype(F32)
    for s in range(4):
        out = nt_dot(by_chip[s], x_rows[...])
        for i, tail in enumerate((zeros, ones, zeros)):
            fulls[s][i * SLOT : (i + 1) * SLOT, :] = jnp.concatenate(
                [out[i * HEAD : (i + 1) * HEAD], tail], axis=0
            ).astype(BF16)


ROWS = 192
TILE = 256


def attention_kernel(at_ref, *refs):
    fulls, others = refs[:4], refs[4:8]
    outs = refs[8:12]
    keys, vals, qry, terms_a, terms_b, found = refs[12:18]
    span = fulls[0].shape[1]
    count = 8 * span
    largest = None
    for c, ref in enumerate(fulls + others):
        block = ref[SLOT : 2 * SLOT, :]
        cols = slice(c * span, (c + 1) * span)
        keys[:SLOT, cols] = block
        keys[SLOT:, cols] = block
        vals[cols, :] = ref[2 * SLOT : 3 * SLOT, :].astype(F32).T.astype(BF16)
        wide = block.astype(F32)
        row = lax.broadcasted_iota(jnp.int32, wide.shape, 0)
        norm = jnp.sum(jnp.where(row < HEAD, wide * wide, 0.0), axis=0, keepdims=True)
        largest = norm if largest is None else jnp.maximum(largest, norm)
    largest = jnp.max(largest, axis=-1, keepdims=True)
    for s in range(4):
        q = fulls[s][0:SLOT, :].astype(F32) * SCORE_SCALE
        high = q.astype(BF16).astype(F32)
        row = lax.broadcasted_iota(jnp.int32, q.shape, 0)
        bound = jnp.sqrt(jnp.sum(q * q, axis=0, keepdims=True) * largest) * (1.0 + 2.0**-6)
        high = jnp.where(row == HEAD, LIFT * math.log(2.0) - bound, high)
        low = jnp.where(row == HEAD, 0.0, q - high)
        both = jnp.concatenate([high, low], axis=0).T
        for a in range(4):
            away = lax.rem(a - at_ref[1] + 4, 4)
            qry[s * 4 + away] = both[a * ROWS : (a + 1) * ROWS].astype(BF16)

    def tile(t):
        return slice(t * TILE, (t + 1) * TILE)

    def fill(q, t, terms, total, shift=None):
        s = jnp.dot(q, keys[:, tile(t)], preferred_element_type=F32)
        e = jnp.exp(s if shift is None else s - shift)
        terms[:, tile(t)] = e
        return total + (e[:, :128] + e[:, 128:])

    def weigh(t, terms, inverse, acc):
        p = (terms[:, tile(t)] * inverse).astype(BF16)
        return acc + jnp.dot(p, vals[tile(t), :], preferred_element_type=F32)

    def put(i, acc):
        found[i] = acc.T[:HEAD].astype(BF16)

    tiles = count // TILE
    none = jnp.zeros((ROWS, 128), F32)
    empty = jnp.zeros((ROWS, SLOT), F32)

    def sums(total):
        total = jnp.sum(total, axis=-1, keepdims=True)
        return total, 1.0 / total

    blocks = qry.shape[0]
    terms_b[...] = jnp.zeros(terms_b.shape, F32)

    def step(i, carry):
        inverse_b, least, most = carry
        one, two = qry[2 * i], qry[2 * i + 1]
        total_a, total_b, acc_a, acc_b = none, none, empty, empty
        for t in range(tiles):
            total_a = fill(one, t, terms_a, total_a)
            acc_b = weigh(t, terms_b, inverse_b, acc_b)
        put(lax.rem(2 * i + blocks, blocks + 1), acc_b)
        total_a, inverse_a = sums(total_a)
        for t in range(tiles):
            total_b = fill(two, t, terms_b, total_b)
            acc_a = weigh(t, terms_a, inverse_a, acc_a)
        put(2 * i, acc_a)
        total_b, inverse_b = sums(total_b)
        return (
            inverse_b,
            jnp.minimum(least, jnp.min(jnp.minimum(total_a, total_b))),
            jnp.maximum(most, jnp.max(jnp.maximum(total_a, total_b))),
        )

    inverse, least, most = lax.fori_loop(
        0,
        blocks // 2,
        step,
        (jnp.zeros((ROWS, 1), F32), jnp.float32(1.0), jnp.float32(1.0)),
    )
    acc = empty
    for t in range(tiles):
        acc = weigh(t, terms_b, inverse, acc)
    put(blocks - 1, acc)
    safe = jnp.logical_and(least > 2.0**-76, most < 2.0**100)

    @pl.when(jnp.logical_not(safe))
    def _():
        def again(i, _):
            q = qry[i].astype(F32)
            lane = lax.broadcasted_iota(jnp.int32, q.shape, 1)
            q = jnp.where(lane == HEAD, 0.0, q).astype(BF16)
            top = None
            for t in range(tiles):
                s = jnp.dot(q, keys[:, tile(t)], preferred_element_type=F32)
                here = jnp.max(s, axis=-1, keepdims=True)
                top = here if top is None else jnp.maximum(top, here)
            total = none
            for t in range(tiles):
                total = fill(q, t, terms_a, total, top)
            inverse = 1.0 / jnp.sum(total, axis=-1, keepdims=True)
            acc = empty
            for t in range(tiles):
                acc = weigh(t, terms_a, inverse, acc)
            put(i, acc)
            return 0

        lax.fori_loop(0, blocks, again, 0)

    for s, out in enumerate(outs):
        out[...] = found[4 * s : 4 * s + 4]


def regroup_kernel(*refs):
    for m, out in enumerate(refs[4:]):
        for s, part in enumerate(refs[:4]):
            out[s] = part[m]


def project_kernel(at_ref, *refs):
    parts = refs[:4]
    wout_ref, wcq_ref, img_ref, gate_ref, after_ref, cq_ref, wide = refs[4:]
    for d, part in enumerate(parts):
        x = lax.rem(at_ref[1] - d + 4, 4)
        for m in range(4):
            side = lax.bitwise_xor(at_ref[0], m)
            head = (side // 2) * 8 + x * 2 + lax.rem(side, 2)
            wide[pl.ds(pl.multiple_of(head * HEAD, 8), HEAD), :] = part[m].astype(F32)
    projected = jnp.dot(wide[...].T.astype(BF16), wout_ref[...], preferred_element_type=F32)
    after = (img_ref[...].astype(F32) + gate_ref[...] * projected).astype(BF16)
    after_ref[...] = after
    cq_ref[...] = jnp.dot(after, wcq_ref[...], preferred_element_type=F32).astype(BF16)


def cross_kernel(len_ref, cq_ref, after_ref, kv_ref, wco_ref, out_ref, wide):
    length = len_ref[0]
    rows = cq_ref.shape[0]
    visible = lax.broadcasted_iota(jnp.int32, (rows, LT), 1) < length
    for h in range(HEADS):
        qry = cq_ref[:, h * HEAD : (h + 1) * HEAD]
        s = jnp.dot(qry, kv_ref[h], preferred_element_type=F32) * SCORE_SCALE
        s = jnp.where(visible, s, -1e30)
        e = jnp.exp(s - jnp.max(s, axis=-1, keepdims=True))
        p = (e / jnp.sum(e, axis=-1, keepdims=True)).astype(BF16)
        wide[h * HEAD : (h + 1) * HEAD, :] = nt_dot(kv_ref[HEADS + h], p)
    final = jnp.dot(wide[...].T.astype(BF16), wco_ref[...], preferred_element_type=F32)
    out_ref[...] = (after_ref[...].astype(F32) + final).astype(BF16)


def whole(dims):
    return pl.BlockSpec(dims, lambda i: (0,) * len(dims))


def third(k):
    return pl.BlockSpec((W, W), lambda i: (0, k))


def project(at, parts, side, img, gate):
    rows = img.shape[0]
    return pl.pallas_call(
        project_kernel,
        grid=(1,),
        out_shape=[shape((rows, W))] * 2,
        in_specs=[SMEM]
        + [whole(part.shape) for part in parts]
        + [third(0), third(1), whole(img.shape), whole(gate.shape)],
        out_specs=[whole((rows, W))] * 2,
        scratch_shapes=[pltpu.VMEM((W, rows), F32)],
        compiler_params=grant(24),
        cost_estimate=pl.CostEstimate(
            flops=4 * rows * W * W, bytes_accessed=8 << 20, transcendentals=0
        ),
        name="project_out_and_query",
    )(at, *parts, side, side, img, gate)


def cross(length, cq, after, kv, side):
    rows = cq.shape[0]
    return pl.pallas_call(
        cross_kernel,
        grid=(1,),
        out_shape=shape((rows, W)),
        in_specs=[SMEM, whole(cq.shape), whole(after.shape), whole(kv.shape), third(2)],
        out_specs=whole((rows, W)),
        scratch_shapes=[pltpu.VMEM((W, rows), F32)],
        compiler_params=grant(16),
        cost_estimate=pl.CostEstimate(
            flops=4 * rows * W * W, bytes_accessed=5 << 20, transcendentals=rows * LT * HEADS
        ),
        name="cross_attention",
    )(length, cq, after, kv, side)


def local(
    token_ids,
    text_lengths,
    embed_table,
    ff_gain,
    wi_gate,
    wi_up,
    wo_down,
    final_gain,
    cap_weight,
    cap_bias,
    image,
    modulation,
    w_qkv,
    w_out,
    w_cq,
    w_ckv,
    w_co,
):
    plane = lax.axis_size(PLANE)
    place = lax.axis_index(PLANE)
    prompts, tokens = token_ids.shape
    share = tokens // plane
    vocab_rows, feats = embed_table.shape
    units = wi_gate.shape[1]
    width = DT // plane

    local_ids = token_ids.reshape(-1) - place * vocab_rows
    one_hot = (local_ids[:, None] == jnp.arange(vocab_rows, dtype=jnp.int32)[None]).astype(BF16)
    picked = jnp.dot(one_hot, embed_table, preferred_element_type=F32).astype(BF16)
    picked = exchange(picked.reshape(plane, -1, feats), PLANE)

    pixels = image[0]
    rows = pixels.shape[0]
    modulate = modulation[0]
    modulated, head_weight = call(
        modulate_kernel,
        "modulate",
        [shape((rows, W)), shape((3 * HEAD, W))],
        (pixels, modulate, w_qkv.T),
    )
    token_blocks = [modulated] + [shifted(modulated, "x", s) for s in range(1, 4)]
    weight_blocks = [head_weight, crossed(head_weight, "core", 1), crossed(head_weight, "yhi", 1)]
    weight_blocks.append(crossed(weight_blocks[2], "core", 1))
    core, row = lax.axis_index("core"), lax.axis_index("tp")
    at = jnp.stack(
        [lax.axis_index(a) for a in (ROW, "x", "tp", PLANE)] + [lax.bitwise_xor(core, row)]
    ).astype(jnp.int32)
    span = 4 * rows
    made = call(
        qkv_kernel,
        "query_key_value",
        [shape((3 * SLOT, span))] * 4,
        (at, *token_blocks, *weight_blocks),
        scratch=[pltpu.VMEM((span, W), BF16), pltpu.VMEM((4, 3 * HEAD, W), BF16)],
        in_specs=[SMEM] + [VMEM] * 8,
        flops=2 * span * W * 12 * HEAD,
        moved=8 << 20,
        mib=56,
    )
    fulls = [made[0]] + [crossed(made[m], ROW, m) for m in range(1, 4)]
    others = [crossed(full, "core", 1) for full in fulls]

    side = call(side_kernel, "side_weights", shape((w_out.shape[0], 3 * W)), (w_out, w_cq, w_co))
    other_side = crossed(side, "tp", 1)
    embedded = call(
        embed_kernel,
        "embed_sum",
        shape(picked.shape),
        (picked,),
        after=(tie(*token_blocks[1:], *weight_blocks[1:3], other_side),),
    )
    gate_up, pair, tick = call(
        gate_up_kernel,
        "text_gate_up",
        [shape((prompts, tokens + 2 * share, 2 * units)), shape((HEAD, 3 * W))],
        (
            at,
            exchange(embedded, PLANE),
            ff_gain.reshape(1, feats),
            wi_gate.T,
            wi_up.T,
            side,
            other_side,
        ),
        scratch=[pltpu.VMEM((feats, 2 * units), BF16), pltpu.VMEM((tokens, feats), F32)],
        in_specs=[SMEM] + [VMEM] * 6,
        flops=4 * prompts * tokens * feats * units,
        moved=4 << 20,
        after=(tie(*fulls[1:], *others),),
        tick=True,
        mib=20,
    )
    side = lax.all_gather(pair, SEQ, axis=0, tiled=True)
    *found, attended = call(
        attention_kernel,
        "self_attention",
        [shape((4, HEAD, rows))] * 4,
        (at, *fulls, *others),
        scratch=[
            pltpu.VMEM((2 * SLOT, 8 * span), BF16),
            pltpu.VMEM((8 * span, SLOT), BF16),
            pltpu.VMEM((16, ROWS, 2 * SLOT), BF16),
            pltpu.VMEM((ROWS, 8 * span), F32),
            pltpu.VMEM((ROWS, 8 * span), F32),
            pltpu.VMEM((17, HEAD, ROWS), BF16),
        ],
        in_specs=[SMEM] + [VMEM] * 8,
        flops=16 * span * 2 * span * 256 * 2,
        moved=8 << 20,
        exps=4 * span * 8 * span,
        after=(tick,),
        tick=True,
        mib=56,
    )
    found = [found[0]] + [crossed(found[m], ROW, m) for m in range(1, 4)]
    down = call(
        down_kernel,
        "text_down",
        shape((plane, tokens + 2 * share, width)),
        (exchange(gate_up, "grp"), wo_down),
        flops=2 * tokens * DT * units,
        moved=5 << 20,
        exps=tokens * units,
        after=(attended,),
    )
    cap_part = call(
        cap_kernel,
        "caption_partial",
        shape((plane, share, W + 128)),
        (exchange(down, PLANE), final_gain.reshape(1, width), cap_weight),
        scratch=[pltpu.VMEM((tokens, width), F32), pltpu.VMEM((tokens, W + 128), F32)],
    )
    *grouped, tick = call(
        regroup_kernel,
        "regroup",
        [shape((4, HEAD, rows))] * 4,
        tuple(found),
        tick=True,
    )
    caption = call(
        caption_kernel,
        "caption",
        shape((plane, share, W)),
        (exchange(cap_part, PLANE), cap_bias.reshape(1, W)),
        after=(tick,),
    )
    parts = [grouped[0]] + [shifted(grouped[d], "x", d) for d in range(1, 4)]
    after_self, cross_query = project(at, parts, side, pixels, modulate[2:3])
    kv_part = call(
        kv_kernel,
        "text_kv",
        shape((plane, w_ckv.shape[1], tokens)),
        (exchange(caption, PLANE), w_ckv.T),
        scratch=[pltpu.VMEM((tokens, W), F32)],
    )
    text_kv = exchange(kv_part, PLANE)
    result = cross(text_lengths, cross_query, after_self, text_kv, side)
    return result[None]


def solution(mesh):
    grp, seq, tp = mesh.devices.shape
    fine = Mesh(mesh.devices.reshape(grp, 2, seq // 4, 2, tp), ("grp",) + PLANE)
    placed = (
        P(),
        P("grp"),
        P(PLANE, "grp"),
        P("grp"),
        P("grp", PLANE),
        P("grp", PLANE),
        P(PLANE, None),
        P(PLANE),
        P(PLANE, None),
        P(),
        P("grp", PLANE, None),
        P("grp", None, None),
        P(None, SEQ),
        P(PLANE, None),
        P(PLANE, None),
        P(None, PLANE),
        P(PLANE, None),
    )
    return jax.shard_map(
        local, mesh=fine, in_specs=placed, out_specs=P("grp", PLANE, None), check_vma=False
    )
```
